512 devices in a mesh: blk: 64 (over z, y_lo, core), rows: 8 (over y_hi, x).
Axes of the slice: x: 4, y: 4 (y_hi: 2, y_lo: 2; y = y_hi * 2 + y_lo), z: 16, core: 2. Of those that a mesh axis runs over, the one named last changes fastest.
Arguments:
- blocks: bfloat16 [64, 8, 3, 64, 4096], P('blk', 'rows'), may hold values from -6 to 6
- block_row: int32 [64, 8, 3], P('blk', 'rows'), may hold values from 0 to 7
- block_col: int32 [64, 8, 3], P('blk', 'rows'), may hold values from 0 to 63
- block_ctx: int32 [64, 8, 3], P('blk', 'rows'), may hold values from 0 to 1
- live_blocks: int32 [64, 8], P('blk', 'rows'), may hold values from 1 to 3, as said below
- user_factor: float32 [32768, 256], P(('blk', 'rows')), may hold values from -2.5 to 2.5
- item_factor: float32 [4096, 256], P('blk'), may hold values from -2.5 to 2.5
- context_factor: float32 [128, 256], replicated, may hold values from -2.5 to 2.5
Outputs:
- new_users: float32 [32768, 256], P(('blk', 'rows'))
- new_items: float32 [4096, 256], P('blk')
- context_grad: float32 [128, 256], replicated
The draws below stay inside these ranges and needn't reach their ends.
Inputs may be any that keep to these rules, and one draw needn't show every extreme that they name: `live_blocks`: every device has at least one used slot; in every draw some device uses all 3 slots.
All inputs are finite; a program needn't handle non-finite values.
Results may differ from the reference program's by a relative error of at most 0.0089.
The reference program's roundings to bfloat16 on the way (of `user_bf`, `pair_vw`, `residual` and `pair_uw`) count: a program that leaves them out, or rounds other values in their place, can miss the bound.
Values may be sent and summed in bfloat16 or wider, within the bound.
A program may use at most 64 MiB of HBM per device.

```python
import math
import jax
import jax.numpy as jnp
from jax import lax

R = 256
BS = 64
NB_DEV = 3
NKB = 2
ITERS = 2
I = 32768
J = 4096
K = 128
N_BLK = 64
N_ROWS = 8


def draw_live_blocks(key, part):
    key_base, key_pick, key_which = jax.random.split(key, 3)
    base_draw = jax.random.randint(key_base, (N_BLK, N_ROWS), 1, NB_DEV + 1)
    pick_draw = jax.random.randint(key_pick, (N_BLK, N_ROWS), 0, 3)
    counts = jnp.where(pick_draw == 0, base_draw, 1)
    which_dev = jax.random.randint(key_which, (), 0, N_BLK * N_ROWS)
    flat_index = jnp.arange(N_BLK * N_ROWS).reshape(N_BLK, N_ROWS)
    return jnp.where(flat_index == which_dev, NB_DEV, counts).astype(jnp.int32)


def place_ends(entries, rng, least, largest):
    place = [jax.random.randint(jax.random.fold_in(rng, axis), (), 0, length) for axis, length in enumerate(entries.shape)]
    main_axis = entries.shape.index(max(entries.shape))
    next_to = place[:main_axis] + [(place[main_axis] + 1) % entries.shape[main_axis]] + place[main_axis + 1:]
    return entries.at[tuple(place)].set(least).at[tuple(next_to)].set(largest)


def level_of(rng, shape, cuts, smallest, largest):
    def one(axis_at, parts):
        draws = jax.random.uniform(jax.random.fold_in(jax.random.fold_in(rng, 6), axis_at), (parts,), jnp.float32, smallest / len(cuts), largest / len(cuts))
        return jnp.repeat(jnp.exp(draws), shape[axis_at] // parts).reshape((-1,) + (1,) * (len(shape) - axis_at - 1))

    gain = one(*cuts[0])
    for cut in cuts[1:]:
        gain = gain * one(*cut)
    return gain


def normal_values(stream_key, dims, deviation, most, cuts=(), held_as=jnp.bfloat16):
    values = jax.random.normal(stream_key, dims, jnp.float32) * deviation
    if len(cuts) > 0:
        values = level_of(stream_key, dims, cuts, -0.22, 0.18) * values
    return jnp.clip(values, min=-most, max=most).astype(held_as)


def setup_inputs(seed: int = 0) -> dict:
    keys = jax.random.split(jax.random.key(seed), 9)
    return {
        "blocks": normal_values(keys[0], (N_BLK, N_ROWS, NB_DEV, BS, BS * BS), 1.0, 6.0, ((0, 64), (1, 8))),
        "block_row": place_ends(jax.random.randint(keys[1], (N_BLK, N_ROWS, NB_DEV), 0, N_ROWS), jax.random.fold_in(keys[1], 1), 0, N_ROWS - 1).astype(jnp.int32),
        "block_col": place_ends(jax.random.randint(keys[2], (N_BLK, N_ROWS, NB_DEV), 0, N_BLK), jax.random.fold_in(keys[2], 1), 0, N_BLK - 1).astype(jnp.int32),
        "block_ctx": place_ends(jax.random.randint(keys[3], (N_BLK, N_ROWS, NB_DEV), 0, NKB), jax.random.fold_in(keys[3], 1), 0, NKB - 1).astype(jnp.int32),
        "live_blocks": draw_live_blocks(jax.random.fold_in(keys[8], 71), 0),
        "user_factor": normal_values(keys[5], (I, R), 0.4, 2.5, ((0, 512),), jnp.float32),
        "item_factor": normal_values(keys[6], (J, R), 0.4, 2.5, ((0, 64),), jnp.float32),
        "context_factor": normal_values(keys[7], (K, R), 0.4, 2.5, (), jnp.float32),
    }


def block_terms(block_x, user_rows, item_rows, context_rows, with_context):
    block_edge = user_rows.shape[0]
    factor_rank = user_rows.shape[1]
    user_wide = user_rows.astype(jnp.float32)
    item_wide = item_rows.astype(jnp.float32)
    context_wide = context_rows.astype(jnp.float32)
    pair_vw = (item_wide[:, None, :] * context_wide[None, :, :]).astype(jnp.bfloat16).reshape(block_edge * block_edge, factor_rank)
    model_block = lax.dot_general(user_rows, pair_vw, (((1,), (1,)), ((), ())), preferred_element_type=jnp.float32)
    residual = (model_block - block_x.astype(jnp.float32)).astype(jnp.bfloat16)
    user_term = jnp.dot(residual, pair_vw, preferred_element_type=jnp.float32)
    pair_uw = (user_wide[:, None, :] * context_wide[None, :, :]).astype(jnp.bfloat16).reshape(block_edge * block_edge, factor_rank)
    resid_items = residual.reshape(block_edge, block_edge, block_edge).transpose(1, 0, 2).reshape(block_edge, block_edge * block_edge)
    item_term = jnp.dot(resid_items, pair_uw, preferred_element_type=jnp.float32)
    if with_context:
        pair_uv = (user_wide[:, None, :] * item_wide[None, :, :]).astype(jnp.bfloat16).reshape(block_edge * block_edge, factor_rank)
        context_term = lax.dot_general(residual.reshape(block_edge * block_edge, block_edge), pair_uv, (((0,), (0,)), ((), ())), preferred_element_type=jnp.float32)
    else:
        context_term = jnp.zeros((block_edge, factor_rank), jnp.float32)
    return (user_term, item_term, context_term)

def add_rows(target, start_row, term):
    current = lax.dynamic_slice_in_dim(target, start_row, term.shape[0], 0)
    return lax.dynamic_update_slice_in_dim(target, current + term, start_row, 0)

def reference(blocks, block_row, block_col, block_ctx, live_blocks, user_factor, item_factor, context_factor):
    block_edge = blocks.shape[3]
    factor_rank = user_factor.shape[1]
    total_slots = N_BLK * N_ROWS * NB_DEV
    flat_blocks = blocks.reshape(total_slots, block_edge, block_edge * block_edge)
    group_base = (jnp.arange(N_BLK, dtype=jnp.int32) * N_ROWS)[:, None, None]
    global_row = (group_base + block_row).reshape(total_slots).astype(jnp.int32)
    item_index = block_col.reshape(total_slots).astype(jnp.int32)
    context_index = block_ctx.reshape(total_slots).astype(jnp.int32)
    alive_flag = (jnp.arange(NB_DEV, dtype=jnp.int32)[None, None, :] < live_blocks[:, :, None]).reshape(total_slots)
    user_step = 6.4 / (block_edge * block_edge)
    item_step = 16.0 / (block_edge * block_edge * N_ROWS)
    grad_scale = 8.0 / (block_edge * math.sqrt(N_BLK * N_ROWS))
    context_grad = jnp.zeros(context_factor.shape, jnp.float32)
    context_bf = context_factor.astype(jnp.bfloat16)
    for step_index in range(ITERS):
        is_last = step_index == ITERS - 1
        user_bf = user_factor.astype(jnp.bfloat16)
        item_bf = item_factor.astype(jnp.bfloat16)

        def visit_block(carried, inputs):
            user_acc, item_acc, ctx_acc = carried
            block_x, row_at, item_at, ctx_at, alive_now = inputs
            user_rows = lax.dynamic_slice_in_dim(user_bf, row_at * block_edge, block_edge, 0)
            item_rows = lax.dynamic_slice_in_dim(item_bf, item_at * block_edge, block_edge, 0)
            context_rows = lax.dynamic_slice_in_dim(context_bf, ctx_at * block_edge, block_edge, 0)
            user_term, item_term, context_term = block_terms(block_x, user_rows, item_rows, context_rows, is_last)
            user_term = jnp.where(alive_now, user_term, 0.0)
            item_term = jnp.where(alive_now, item_term, 0.0)
            context_term = jnp.where(alive_now, context_term, 0.0)
            user_acc = add_rows(user_acc, row_at * block_edge, user_term)
            item_acc = add_rows(item_acc, item_at * block_edge, item_term)
            ctx_acc = add_rows(ctx_acc, ctx_at * block_edge, context_term)
            return ((user_acc, item_acc, ctx_acc), None)
        start_acc = (jnp.zeros(user_factor.shape, jnp.float32), jnp.zeros(item_factor.shape, jnp.float32), jnp.zeros(context_factor.shape, jnp.float32))
        sums, _ = lax.scan(visit_block, start_acc, (flat_blocks, global_row, item_index, context_index, alive_flag))
        user_factor = user_factor - user_step * sums[0]
        item_factor = item_factor - item_step * sums[1]
        if is_last:
            context_grad = sums[2] * grad_scale
    return (user_factor, item_factor, context_grad)
```

```python
import functools
import math

import jax
import jax.numpy as jnp
from jax import lax
from jax.experimental import pallas as pl
from jax.experimental.pallas import tpu as pltpu
from jax.sharding import PartitionSpec as P

ITERS = 2
NQ = 4
MESH = pl.DeviceIdType.MESH
F32 = jnp.float32
BF16 = jnp.bfloat16


def stack_halves(x):
    return jnp.concatenate([x[..., :128], x[..., 128:]], axis=-2)


def unstack_halves(x):
    n = x.shape[-2] // 2
    return jnp.concatenate([x[..., :n, :], x[..., n:, :]], axis=-1)


class Exchange:
    def __init__(self, n, me, dev, src, land, send, recv):
        self.n, self.me, self.dev, self.src, self.land = n, me, dev, src, land
        self.send, self.recv = send, recv

    def _copy(self, step):
        to = lax.rem(self.me + step, self.n)
        return pltpu.make_async_remote_copy(
            src_ref=self.src(to),
            dst_ref=self.land(self.me),
            send_sem=self.send.at[step - 1],
            recv_sem=self.recv.at[step - 1],
            device_id=self.dev(to),
            device_id_type=MESH,
        )

    def _arrival(self, step):
        frm = lax.rem(self.me + self.n - step, self.n)
        return pltpu.make_async_remote_copy(
            src_ref=self.land(frm),
            dst_ref=self.land(frm),
            send_sem=self.send.at[step - 1],
            recv_sem=self.recv.at[step - 1],
            device_id=self.dev(frm),
            device_id_type=MESH,
        )

    def start(self):
        @pl.loop(1, self.n)
        def _(step):
            self._copy(step).start()

    def wait(self):
        @pl.loop(1, self.n)
        def _(step):
            self._arrival(step).wait_recv()

    def finish(self):
        @pl.loop(1, self.n)
        def _(step):
            self._copy(step).wait_send()


def kernel(
    nz, nr, user_step, item_step, grad_scale,
    blocks, row_of, col_of, ctx_of, live_of, user_in, item_in, ctx_in,
    new_users, new_items, ctx_out,
    xb, gu, idx, bmat, amat, zg, qg, ys, rg, vf, wf, ub, user_t, item_t, ctx_t,
    xs0, xr0, xs1, xr1, us, ur, qs, qr, zs, zr, cqs, cqr, cz, cq2, fin,
    xsem, rsend, rrecv, qsend, qrecv, zsend, zrecv,
):
    blk = lax.axis_index("blk")
    r = lax.axis_index("rows")
    z, q = blk // NQ, lax.rem(blk, NQ)
    slots = xb.shape[0]
    nb = nz * NQ

    def row_dev(i):
        return (blk, i)

    def q_dev(i):
        return (z * NQ + i, r)

    def z_dev(i):
        return (i * NQ + q, r)

    pending = []
    used = {"r": 0, "q": 0, "z": 0}

    def exchange(kind, src, land):
        n, me, dev, send, recv = {
            "r": (nr, r, row_dev, rsend, rrecv),
            "q": (NQ, q, q_dev, qsend, qrecv),
            "z": (nz, z, z_dev, zsend, zrecv),
        }[kind]
        at = used[kind]
        used[kind] += 1
        e = Exchange(n, me, dev, src, land, send.at[at], recv.at[at])
        e.start()
        pending.append(e)
        return e

    load = pltpu.make_async_copy(blocks.at[0, 0], xb, xsem)
    load.start()

    barrier = pltpu.get_barrier_semaphore()
    for n, me, dev in ((nr, r, row_dev), (NQ, q, q_dev), (nz, z, z_dev)):

        @pl.loop(1, n)
        def _(step):
            pl.semaphore_signal(
                barrier, inc=1, device_id=dev(lax.rem(me + step, n)), device_id_type=MESH
            )

    live = live_of[0, 0]
    rows = [row_of[0, 0, s] for s in range(slots)]
    ctxs = [ctx_of[0, 0, s] for s in range(slots)]
    alive = [(s < live).astype(jnp.int32) for s in range(slots)]

    i16 = lax.broadcasted_iota(jnp.int32, (16, 128), 0)
    for s in range(slots):
        col = col_of[0, 0, s]
        place = ((col & (NQ - 1)) * nz + (col >> 2)) * 16
        target = (i16 + place) * alive[s] + (alive[s] - 1)
        idx[r, pl.ds(16 * s, 16), :] = target

    user_own = user_in[...]
    item_own = stack_halves(item_in[pl.ds(pl.multiple_of(r * 8, 8), 8), :])
    gu[0, r] = user_own.astype(BF16)
    zg[0, z] = item_own.astype(BF16)
    for s in range(slots):
        w = ctx_in[...].astype(BF16).astype(F32)
        second = ctxs[s].astype(F32)
        wf[s] = w[:64] * (1.0 - second) + w[64:] * second

    pl.semaphore_wait(barrier, nr - 1 + NQ - 1 + nz - 1)

    for k in range(ITERS):
        last = k == ITERS - 1
        z_gather = exchange("z", lambda i, k=k: zg.at[k, z], lambda i, k=k: zg.at[k, i])
        if k == 0:
            index_gather = exchange("r", lambda i: idx.at[r], lambda i: idx.at[i])
            user_gather = exchange("r", lambda i: gu.at[0, r], lambda i: gu.at[0, i])
        z_gather.wait()
        qg[k, q] = zg[k]
        q_gather = exchange("q", lambda i, k=k: zg.at[k], lambda i, k=k: qg.at[k, i])
        if k == 0:
            index_gather.wait()
            wanted = idx[...].reshape(nr * slots * 16, 128)
            count = nr * slots * 16
            lane = lax.broadcasted_iota(jnp.int32, (count, 128), 1)
            for c in range(nb * 16 // 128):
                hit = jnp.where(lane + 128 * c == wanted, 1.0, 0.0)
                bmat[:, 128 * c : 128 * (c + 1)] = hit.astype(BF16)
            row16 = lax.broadcasted_iota(jnp.int32, (nb * 16, 128), 0)
            i0 = lax.broadcasted_iota(jnp.int32, (128, 128), 0)
            i1 = lax.broadcasted_iota(jnp.int32, (128, 128), 1)
            for c in range(count // 128):
                part = jnp.where(i0 == i1, wanted[128 * c : 128 * (c + 1)], 0)
                along = jnp.sum(part, axis=0, keepdims=True)
                hit = jnp.where(row16 == along, 1.0, 0.0)
                amat[:, 128 * c : 128 * (c + 1)] = hit.astype(BF16)
        q_gather.wait()
        shares = qg[k].reshape(nb * 16, 128)
        picked = jnp.dot(bmat[...], shares, preferred_element_type=F32)
        ys[k] = picked.astype(BF16).reshape(nr, slots * 16, 128)
        rg[k, r] = ys[k, r]
        item_answer = exchange("r", lambda i, k=k: ys.at[k, i], lambda i, k=k: rg.at[k, i])
        user_gather.wait()
        for s in range(slots):
            total = jnp.zeros((64, 256), F32)
            for p in range(nr):
                total += gu[k, p].astype(F32) * (rows[s] == p).astype(jnp.int32).astype(F32)
            ub[s] = total.astype(BF16)
        item_answer.wait()
        for s in range(slots):
            part = rg[k, :, pl.ds(16 * s, 16), :].astype(F32)
            vf[s] = unstack_halves(part).reshape(64, 256)
        if k == 0:
            load.wait()
        user_t[...] = jnp.zeros_like(user_t)
        if last:
            ctx_t[...] = jnp.zeros_like(ctx_t)

        @pl.loop(0, 8)
        def _(c):
            for s in range(slots):
                u, w = ub[s], wf[s]
                v = vf[s, pl.ds(pl.multiple_of(c * 8, 8), 8), :]
                pair = (v[:, None, :] * w[None, :, :]).astype(BF16).reshape(512, 256)
                model = lax.dot_general(
                    u, pair, (((1,), (1,)), ((), ())), preferred_element_type=F32
                )
                x = xb[s, :, pl.ds(pl.multiple_of(c * 512, 512), 512)]
                resid = (model - x.astype(F32)).astype(BF16)
                user_t[s] += jnp.dot(resid, pair, preferred_element_type=F32)
                g = lax.dot_general(
                    resid, u, (((0,), (0,)), ((), ())), preferred_element_type=F32
                ).reshape(8, 64, 256)
                item_t[s, pl.ds(pl.multiple_of(c * 8, 8), 8), :] = jnp.sum(g * w[None], axis=1)
                if last:
                    ctx_t[s] += jnp.sum(g * v[:, None, :], axis=0)

        xs, xr = (xs1, xr1) if last else (xs0, xr0)
        for s in range(slots):
            tile = item_t[s].reshape(nr, 8, 256)
            xs[:, pl.ds(16 * s, 16), :] = stack_halves(tile).astype(BF16)
        if last:
            for c in range(2):
                total = jnp.zeros((64, 256), F32)
                for s in range(slots):
                    mine = alive[s] * (ctxs[s] == c).astype(jnp.int32)
                    total += ctx_t[s] * mine.astype(F32)
                tile = stack_halves(total.reshape(nr, 8, 256))
                xs[:, pl.ds(16 * (slots + c), 16), :] = tile.astype(BF16)
        xr[r] = xs[r]
        item_parts = exchange("r", lambda i, xs=xs: xs.at[i], lambda i, xr=xr: xr.at[i])
        for p in range(nr):
            total = jnp.zeros((64, 256), F32)
            for s in range(slots):
                mine = alive[s] * (rows[s] == p).astype(jnp.int32)
                total += user_t[s] * mine.astype(F32)
            us[k, p] = total.astype(BF16)
        ur[k, r] = us[k, r]
        user_parts = exchange("r", lambda i, k=k: us.at[k, i], lambda i, k=k: ur.at[k, i])

        item_parts.wait()
        parts = xr[:, : slots * 16, :].reshape(nr * slots * 16, 128)
        summed = jnp.dot(amat[...], parts, preferred_element_type=F32)
        qs[k] = summed.astype(BF16).reshape(NQ, nz, 16, 128)
        qr[k, q] = qs[k, q]
        q_parts = exchange("q", lambda i, k=k: qs.at[k, i], lambda i, k=k: qr.at[k, i])
        if last:
            total = jnp.sum(xr[:, slots * 16 :, :].astype(F32), axis=0)
            cqs[...] = total.reshape(NQ, 8, 128)
            cqr[q] = cqs[q]
            ctx_q = exchange("q", lambda i: cqs.at[i], lambda i: cqr.at[i])
        user_parts.wait()
        user_own = user_own - user_step * jnp.sum(ur[k].astype(F32), axis=0)
        if last:
            new_users[...] = user_own
        else:
            gu[k + 1, r] = user_own.astype(BF16)
            user_gather = exchange(
                "r", lambda i, k=k: gu.at[k + 1, r], lambda i, k=k: gu.at[k + 1, i]
            )
        q_parts.wait()
        zs[k] = jnp.sum(qr[k].astype(F32), axis=0).astype(BF16)
        zr[k, z] = zs[k, z]
        z_parts = exchange("z", lambda i, k=k: zs.at[k, i], lambda i, k=k: zr.at[k, i])
        if last:
            ctx_q.wait()
            cz[z] = jnp.sum(cqr[...], axis=0)
            ctx_z = exchange("z", lambda i: cz.at[z], lambda i: cz.at[i])
        z_parts.wait()
        item_own = item_own - item_step * jnp.sum(zr[k].astype(F32), axis=0)
        if not last:
            zg[k + 1, z] = item_own.astype(BF16)

    ctx_z.wait()
    cq2[q] = jnp.sum(cz[...], axis=0) * grad_scale
    ctx_gather = exchange("q", lambda i: cq2.at[q], lambda i: cq2.at[i])
    ctx_gather.wait()
    fin[r, pl.ds(0, 16), :] = item_own
    fin[r, pl.ds(16, 32), :] = cq2[...].reshape(32, 128)
    last_gather = exchange("r", lambda i: fin.at[r], lambda i: fin.at[i])
    last_gather.wait()
    new_items[...] = unstack_halves(fin[:, :16, :]).reshape(64, 256)
    for c in range(2):
        part = fin[:, pl.ds(16 + 16 * c, 16), :]
        ctx_out[pl.ds(64 * c, 64), :] = unstack_halves(part).reshape(64, 256)
    for e in pending:
        e.finish()


def local(
    blocks, block_row, block_col, block_ctx, live_blocks, user_factor, item_factor, context_factor
):
    nr = lax.axis_size("rows")
    nz = lax.axis_size("blk") // NQ
    slots = blocks.shape[2]
    nb = nz * NQ
    edge = blocks.shape[3]
    vm = pltpu.VMEM
    dma = pltpu.SemaphoreType.DMA
    scratch = [
        vm((slots, 64, 4096), BF16),
        vm((ITERS, nr, 64, 256), BF16),
        vm((nr, slots * 16, 128), jnp.int32),
        vm((nr * slots * 16, nb * 16), BF16),
        vm((nb * 16, nr * slots * 16), BF16),
        vm((ITERS, nz, 16, 128), BF16),
        vm((ITERS, NQ, nz, 16, 128), BF16),
        vm((ITERS, nr, slots * 16, 128), BF16),
        vm((ITERS, nr, slots * 16, 128), BF16),
        vm((slots, 64, 256), F32),
        vm((slots, 64, 256), F32),
        vm((slots, 64, 256), BF16),
        vm((slots, 64, 256), F32),
        vm((slots, 64, 256), F32),
        vm((slots, 64, 256), F32),
        vm((nr, slots * 16, 128), BF16),
        vm((nr, slots * 16, 128), BF16),
        vm((nr, slots * 16 + 32, 128), BF16),
        vm((nr, slots * 16 + 32, 128), BF16),
        vm((ITERS, nr, 64, 256), BF16),
        vm((ITERS, nr, 64, 256), BF16),
        vm((ITERS, NQ, nz, 16, 128), BF16),
        vm((ITERS, NQ, nz, 16, 128), BF16),
        vm((ITERS, nz, 16, 128), BF16),
        vm((ITERS, nz, 16, 128), BF16),
        vm((NQ, 8, 128), F32),
        vm((NQ, 8, 128), F32),
        vm((nz, 8, 128), F32),
        vm((NQ, 8, 128), F32),
        vm((nr, 48, 128), F32),
        dma,
        dma((10, nr - 1)),
        dma((10, nr - 1)),
        dma((6, NQ - 1)),
        dma((6, NQ - 1)),
        dma((5, nz - 1)),
        dma((5, nz - 1)),
    ]
    body = functools.partial(
        kernel,
        nz,
        nr,
        6.4 / (edge * edge),
        16.0 / (edge * edge * nr),
        8.0 / (edge * math.sqrt(nb * nr)),
    )
    in_vmem = pl.BlockSpec(memory_space=pltpu.VMEM)
    in_smem = pl.BlockSpec(memory_space=pltpu.SMEM)
    return pl.pallas_call(
        body,
        out_shape=(
            jax.ShapeDtypeStruct(user_factor.shape, F32),
            jax.ShapeDtypeStruct(item_factor.shape, F32),
            jax.ShapeDtypeStruct(context_factor.shape, F32),
        ),
        in_specs=[pl.BlockSpec(memory_space=pl.ANY)] + [in_smem] * 4 + [in_vmem] * 3,
        out_specs=(in_vmem,) * 3,
        scratch_shapes=scratch,
        compiler_params=pltpu.CompilerParams(
            collective_id=0, has_side_effects=True, vmem_limit_bytes=40 * 1024 * 1024
        ),
    )(
        blocks, block_row, block_col, block_ctx, live_blocks,
        user_factor, item_factor, context_factor,
    )


def solution(mesh):
    return jax.shard_map(
        local,
        mesh=mesh,
        in_specs=(
            P("blk", "rows", None, None, None),
            P("blk", "rows", None),
            P("blk", "rows", None),
            P("blk", "rows", None),
            P("blk", "rows"),
            P(("blk", "rows"), None),
            P("blk", None),
            P(),
        ),
        out_specs=(P(("blk", "rows"), None), P("blk", None), P()),
        check_vma=False,
    )
```

```python
import functools
import math

import jax
import jax.numpy as jnp
from jax import lax
from jax.experimental import pallas as pl
from jax.experimental.pallas import tpu as pltpu
from jax.sharding import PartitionSpec as P

ITERS = 2
NQ = 4
MESH = pl.DeviceIdType.MESH
F32 = jnp.float32
BF16 = jnp.bfloat16


class Exchange:
    def __init__(self, group, src, land, send, recv):
        self.steps, self.me, self.peer, self.source, self.dev = group
        self.src, self.land, self.send, self.recv = src, land, send, recv

    def _copy(self, i):
        to = self.peer(i)
        return pltpu.make_async_remote_copy(
            src_ref=self.src(to),
            dst_ref=self.land(self.me),
            send_sem=self.send.at[i],
            recv_sem=self.recv.at[i],
            device_id=self.dev(to),
            device_id_type=MESH,
        )

    def _arrival(self, i):
        frm = self.source(i)
        return pltpu.make_async_remote_copy(
            src_ref=self.land(frm),
            dst_ref=self.land(frm),
            send_sem=self.send.at[i],
            recv_sem=self.recv.at[i],
            device_id=self.dev(frm),
            device_id_type=MESH,
        )

    def start(self):
        @pl.loop(0, self.steps)
        def _(i):
            self._copy(i).start()

    def wait(self):
        @pl.loop(0, self.steps)
        def _(i):
            self._arrival(i).wait_recv()

    def finish(self):
        @pl.loop(0, self.steps)
        def _(i):
            self._copy(i).wait_send()


def ring(n, me, dev, far_first):
    def offset(i):
        if not far_first:
            return i + 1
        return n // 2 + (1 - 2 * (i % 2)) * ((i + 1) // 2)

    return (
        n - 1,
        me,
        lambda i: lax.rem(me + offset(i), n),
        lambda i: lax.rem(me + n - offset(i), n),
        dev,
    )


def plane(nr, q, r, dev):
    y_lo, core, y_hi, x = q // 2, lax.rem(q, 2), r // 4, lax.rem(r, 4)
    n = NQ * nr

    def member(i, sign):
        t = n - 1 - i
        b = (t // 4) % 4
        dx = (3 * b + 3 * (b // 2) - 2 * (b // 3)) % 4
        to_x = lax.rem(x + 4 + sign * dx, 4)
        to_hi = lax.rem(y_hi + t // 16, 2)
        to_lo = lax.rem(y_lo + (t // 2) % 2, 2)
        to_core = lax.rem(core + t % 2, 2)
        return (to_lo * 2 + to_core) * nr + to_hi * 4 + to_x

    return (n - 1, q * nr + r, lambda i: member(i, 1), lambda i: member(i, -1), dev)


def to_tiles(x):
    y = x.reshape(8, 8, 256)
    return jnp.stack([y[..., :128], y[..., 128:]], axis=1).reshape(16, 8, 128)


def from_tiles(x):
    y = x.reshape(8, 2, 8, 128)
    return jnp.concatenate([y[:, 0], y[:, 1]], axis=-1).reshape(64, 256)


def join_shares(x):
    y = x.reshape(16, 2, 4, 128)
    return from_tiles(jnp.concatenate([y[:, 0], y[:, 1]], axis=1))


def kernel(
    nz, nr, user_step, item_step, grad_scale,
    blocks, row_hbm, col_hbm, ctx_hbm, live_hbm, user_hbm, item_hbm, factor_hbm,
    new_users, new_items, ctx_out,
    xb, gu, idx, bmat, amat, iq, ist, zg, ys, rg, vf, wf, ub, user_t, item_t, ctx_t,
    xs0, xr0, xs1, xr1, us, ur, zs, zr, cz, fs, fin,
    row_of, col_of, ctx_of, live_of, user_in, item_in, ctx_in, insem,
    xsem, rsend, rrecv, qsend, qrecv, zsend, zrecv, psend, precv,
):
    blk = lax.axis_index("blk")
    r = lax.axis_index("rows")
    z, q = blk // NQ, lax.rem(blk, NQ)
    me = q * nr + r
    slots = xb.shape[0]
    members = NQ * nr
    groups = {
        "r": ring(nr, r, lambda i: (blk, i), False),
        "q": ring(NQ, q, lambda i: (z * NQ + i, r), False),
        "z": ring(nz, z, lambda i: (i * NQ + q, r), True),
        "p": plane(nr, q, r, lambda i: (z * NQ + i // nr, lax.rem(i, nr))),
    }
    semaphores = {
        "r": (rsend, rrecv), "q": (qsend, qrecv), "z": (zsend, zrecv), "p": (psend, precv),
    }

    pending = []
    used = {"r": 0, "q": 0, "z": 0, "p": 0}

    def exchange(kind, src, land):
        send, recv = semaphores[kind]
        at = used[kind]
        used[kind] += 1
        e = Exchange(groups[kind], src, land, send.at[at], recv.at[at])
        e.start()
        pending.append(e)
        return e

    barrier = pltpu.get_barrier_semaphore()
    for kind in ("z", "p"):
        steps, _, peer, _, dev = groups[kind]

        @pl.loop(0, steps)
        def _(i):
            pl.semaphore_signal(
                barrier, inc=1, device_id=dev(peer(i)), device_id_type=MESH
            )

    inputs = [
        pltpu.make_async_copy(src, dst, insem.at[i])
        for i, (src, dst) in enumerate(
            (
                (item_hbm, item_in),
                (live_hbm, live_of),
                (col_hbm, col_of),
                (user_hbm, user_in),
                (row_hbm, row_of),
                (ctx_hbm, ctx_of),
                (factor_hbm, ctx_in),
            )
        )
    ]
    for c in inputs:
        c.start()
    load = pltpu.make_async_copy(blocks.at[0, 0], xb, xsem)
    load.start()
    for c in inputs:
        c.wait()
    live = live_of[0, 0]
    rows = [row_of[0, 0, s] for s in range(slots)]
    ctxs = [ctx_of[0, 0, s] for s in range(slots)]
    alive = [(s < live).astype(jnp.int32) for s in range(slots)]

    item_tiles = to_tiles(item_in[...])
    halves = [item_tiles, jnp.concatenate([item_tiles[:, 4:], item_tiles[:, :4]], axis=1)]
    ist[...] = jnp.stack(halves, axis=1).reshape(members, 8, 128)
    iq[q] = ist[me]
    sub = lax.broadcasted_iota(jnp.int32, (8, 128), 0)
    start = jnp.full((8, 128), -1000, jnp.int32)
    for s in range(slots):
        at = (col_of[0, 0, s] * 4) * alive[s] - 1000 * (1 - alive[s])
        start = jnp.where(sub == s, at, start)
    idx[me] = start
    user_own = user_in[...]
    gu[0, r] = user_own.astype(BF16)

    pl.semaphore_wait(barrier, nz - 1 + members - 1)

    item_first = exchange("q", lambda i: ist.at[i * nr + r], lambda i: iq.at[i])
    index_gather = exchange("p", lambda i: idx.at[me], lambda i: idx.at[i])
    item_first.wait()
    item_own = jnp.concatenate([iq[i][:4] for i in range(NQ)], axis=0)
    item_delta = jnp.zeros((16, 128), F32)
    zg[0, z] = item_own.astype(BF16)

    for k in range(ITERS):
        last = k == ITERS - 1
        z_gather = exchange("z", lambda i, k=k: zg.at[k, z], lambda i, k=k: zg.at[k, i])
        if k == 0:
            user_gather = exchange("r", lambda i: gu.at[0, r], lambda i: gu.at[0, i])
            for s in range(slots):
                w = ctx_in[...].astype(BF16).astype(F32)
                second = ctxs[s].astype(F32)
                wf[s] = w[:64] * (1.0 - second) + w[64:] * second
            index_gather.wait()
            sub3 = lax.broadcasted_iota(jnp.int32, (members, 8, 128), 1)
            row = [
                jnp.broadcast_to(idx[:, pl.ds(s, 1), :], (members, 8, 128)) for s in range(slots)
            ]
            first = jnp.where(sub3 < 4, row[0], row[1]) + lax.rem(sub3, 4)
            second = jnp.where(sub3 < 4, row[2], -1000) + lax.rem(sub3, 4)
            count = members * 16
            wanted = jnp.concatenate([first, second], axis=1).reshape(count, 128)
            total_rows = nz * 16
            lane = lax.broadcasted_iota(jnp.int32, (count, 128), 1)
            for c in range(total_rows // 128):
                hit = jnp.where(lane + 128 * c == wanted, 1.0, 0.0)
                bmat[:, 128 * c : 128 * (c + 1)] = hit.astype(BF16)
            at_row = lax.broadcasted_iota(jnp.int32, (total_rows, 128), 0)
            i0 = lax.broadcasted_iota(jnp.int32, (128, 128), 0)
            i1 = lax.broadcasted_iota(jnp.int32, (128, 128), 1)
            for c in range(count // 128):
                part = jnp.where(i0 == i1, wanted[128 * c : 128 * (c + 1)], 0)
                along = jnp.sum(part, axis=0, keepdims=True)
                hit = jnp.where(at_row == along, 1.0, 0.0)
                amat[:, 128 * c : 128 * (c + 1)] = hit.astype(BF16)
        z_gather.wait()
        shares = zg[k].reshape(nz * 16, 128)
        picked = jnp.dot(bmat[...], shares, preferred_element_type=F32)
        ys[k] = picked.astype(BF16).reshape(members, 16, 128)
        rg[k, me] = ys[k, me]
        answer = exchange("p", lambda i, k=k: ys.at[k, i], lambda i, k=k: rg.at[k, i])
        user_gather.wait()
        for s in range(slots):
            total = jnp.zeros((64, 256), F32)
            for p in range(nr):
                total += gu[k, p].astype(F32) * (rows[s] == p).astype(jnp.int32).astype(F32)
            ub[s] = total.astype(BF16)
        user_t[...] = jnp.zeros_like(user_t)
        if last:
            ctx_t[...] = jnp.zeros_like(ctx_t)
        else:
            load.wait()
        answer.wait()
        got = rg[k].astype(F32)
        for s in range(slots):
            vf[s] = join_shares(got[:, 4 * s : 4 * s + 4, :])

        @pl.loop(0, 8)
        def _(c):
            for s in range(slots):
                u, w = ub[s], wf[s]
                v = vf[s, pl.ds(pl.multiple_of(c * 8, 8), 8), :]
                pair = (v[:, None, :] * w[None, :, :]).astype(BF16).reshape(512, 256)
                model = lax.dot_general(
                    u, pair, (((1,), (1,)), ((), ())), preferred_element_type=F32
                )
                x = xb[s, :, pl.ds(pl.multiple_of(c * 512, 512), 512)]
                resid = (model - x.astype(F32)).astype(BF16)
                user_t[s] += jnp.dot(resid, pair, preferred_element_type=F32)
                g = lax.dot_general(
                    resid, u, (((0,), (0,)), ((), ())), preferred_element_type=F32
                ).reshape(8, 64, 256)
                item_t[s, pl.ds(pl.multiple_of(c * 8, 8), 8), :] = jnp.sum(g * w[None], axis=1)
                if last:
                    ctx_t[s] += jnp.sum(g * v[:, None, :], axis=0)

        xs, xr = (xs1, xr1) if last else (xs0, xr0)
        tiles = [to_tiles(item_t[s]) for s in range(slots)]
        fill = jnp.zeros((16, 4, 128), F32)
        for half in range(2):
            cut = [t[:, 4 * half : 4 * half + 4] for t in tiles]
            part = jnp.concatenate(cut + [fill], axis=1).astype(BF16)
            for v in range(16):
                xs[2 * v + half, pl.ds(0, 16), :] = part[v]
        if last:
            for c in range(2):
                total = jnp.zeros((64, 256), F32)
                for s in range(slots):
                    mine = alive[s] * (ctxs[s] == c).astype(jnp.int32)
                    total += ctx_t[s] * mine.astype(F32)
                part = to_tiles(total)
                part = jnp.concatenate([part, jnp.zeros_like(part)], axis=1).astype(BF16)
                xs[pl.ds(16 * c, 16), pl.ds(16, 16), :] = part
        xr[me] = xs[me]
        item_parts = exchange("p", lambda i, xs=xs: xs.at[i], lambda i, xr=xr: xr.at[i])
        for p in range(nr):
            total = jnp.zeros((64, 256), F32)
            for s in range(slots):
                mine = alive[s] * (rows[s] == p).astype(jnp.int32)
                total += user_t[s] * mine.astype(F32)
            us[k, p] = total.astype(BF16)
        ur[k, r] = us[k, r]
        user_parts = exchange("r", lambda i, k=k: us.at[k, i], lambda i, k=k: ur.at[k, i])

        item_parts.wait()
        parts = xr[:, :16, :].reshape(members * 16, 128)
        summed = jnp.dot(amat[...], parts, preferred_element_type=F32)
        zs[k] = summed.astype(BF16).reshape(nz, 16, 128)
        zr[k, z] = zs[k, z]
        z_parts = exchange("z", lambda i, k=k: zs.at[k, i], lambda i, k=k: zr.at[k, i])
        if last:
            cz[z] = jnp.sum(xr[:, 16:, :].astype(F32), axis=0)[:8]
            ctx_z = exchange("z", lambda i: cz.at[z], lambda i: cz.at[i])
        user_parts.wait()
        user_own = user_own - user_step * jnp.sum(ur[k].astype(F32), axis=0)
        if last:
            new_users[...] = user_own
        else:
            gu[k + 1, r] = user_own.astype(BF16)
            user_gather = exchange(
                "r", lambda i, k=k: gu.at[k + 1, r], lambda i, k=k: gu.at[k + 1, i]
            )
        z_parts.wait()
        item_delta = item_delta + item_step * jnp.sum(zr[k].astype(F32), axis=0)
        if not last:
            zg[k + 1, z] = (item_own - item_delta).astype(BF16)

    ctx_z.wait()
    ctx_share = jnp.sum(cz[...], axis=0) * grad_scale
    for i in range(NQ):
        part = item_delta[4 * i : 4 * i + 4]
        fs[i] = jnp.concatenate([part, part, ctx_share], axis=0).astype(BF16)
    fin[me] = fs[q]
    final = exchange("p", lambda i: fs.at[i // nr], lambda i: fin.at[i])
    final.wait()
    got = fin[...].astype(F32)
    new_items[...] = item_in[...] - join_shares(got[:, :4])
    for c in range(2):
        ctx_out[pl.ds(64 * c, 64), :] = from_tiles(got[16 * c : 16 * c + 16, 8:])
    for e in pending:
        e.finish()


def local(
    blocks, block_row, block_col, block_ctx, live_blocks, user_factor, item_factor, context_factor
):
    nr = lax.axis_size("rows")
    nz = lax.axis_size("blk") // NQ
    slots = blocks.shape[2]
    nb = nz * NQ
    edge = blocks.shape[3]
    vm = pltpu.VMEM
    dma = pltpu.SemaphoreType.DMA
    members = NQ * nr
    scratch = [
        vm((slots, 64, 4096), BF16),
        vm((ITERS, nr, 64, 256), BF16),
        vm((members, 8, 128), jnp.int32),
        vm((members * 16, nz * 16), BF16),
        vm((nz * 16, members * 16), BF16),
        vm((NQ, 8, 128), F32),
        vm((members, 8, 128), F32),
        vm((ITERS, nz, 16, 128), BF16),
        vm((ITERS, members, 16, 128), BF16),
        vm((ITERS, members, 16, 128), BF16),
        vm((slots, 64, 256), F32),
        vm((slots, 64, 256), F32),
        vm((slots, 64, 256), BF16),
        vm((slots, 64, 256), F32),
        vm((slots, 64, 256), F32),
        vm((slots, 64, 256), F32),
        vm((members, 16, 128), BF16),
        vm((members, 16, 128), BF16),
        vm((members, 32, 128), BF16),
        vm((members, 32, 128), BF16),
        vm((ITERS, nr, 64, 256), BF16),
        vm((ITERS, nr, 64, 256), BF16),
        vm((ITERS, nz, 16, 128), BF16),
        vm((ITERS, nz, 16, 128), BF16),
        vm((nz, 8, 128), F32),
        vm((NQ, 16, 128), BF16),
        vm((members, 16, 128), BF16),
        pltpu.SMEM((1, 1, slots), jnp.int32),
        pltpu.SMEM((1, 1, slots), jnp.int32),
        pltpu.SMEM((1, 1, slots), jnp.int32),
        pltpu.SMEM((1, 1), jnp.int32),
        vm((64, 256), F32),
        vm((64, 256), F32),
        vm((128, 256), F32),
        dma((7,)),
        dma,
        dma((4, nr - 1)),
        dma((4, nr - 1)),
        dma((1, NQ - 1)),
        dma((1, NQ - 1)),
        dma((5, nz - 1)),
        dma((5, nz - 1)),
        dma((6, members - 1)),
        dma((6, members - 1)),
    ]
    body = functools.partial(
        kernel,
        nz,
        nr,
        6.4 / (edge * edge),
        16.0 / (edge * edge * nr),
        8.0 / (edge * math.sqrt(nb * nr)),
    )
    in_vmem = pl.BlockSpec(memory_space=pltpu.VMEM)
    return pl.pallas_call(
        body,
        out_shape=(
            jax.ShapeDtypeStruct(user_factor.shape, F32),
            jax.ShapeDtypeStruct(item_factor.shape, F32),
            jax.ShapeDtypeStruct(context_factor.shape, F32),
        ),
        in_specs=[pl.BlockSpec(memory_space=pltpu.HBM)] * 8,
        out_specs=(in_vmem,) * 3,
        scratch_shapes=scratch,
        compiler_params=pltpu.CompilerParams(
            collective_id=0, has_side_effects=True, vmem_limit_bytes=56 * 1024 * 1024
        ),
    )(
        blocks, block_row, block_col, block_ctx, live_blocks,
        user_factor, item_factor, context_factor,
    )


def solution(mesh):
    return jax.shard_map(
        local,
        mesh=mesh,
        in_specs=(
            P("blk", "rows", None, None, None),
            P("blk", "rows", None),
            P("blk", "rows", None),
            P("blk", "rows", None),
            P("blk", "rows"),
            P(("blk", "rows"), None),
            P("blk", None),
            P(),
        ),
        out_specs=(P(("blk", "rows"), None), P("blk", None), P()),
        check_vma=False,
    )
```

```python
import functools
import math

import jax
import jax.numpy as jnp
from jax import lax
from jax.experimental import pallas as pl
from jax.experimental.pallas import tpu as pltpu
from jax.sharding import PartitionSpec as P

ITERS = 2
NQ = 4
MESH = pl.DeviceIdType.MESH
F32 = jnp.float32
BF16 = jnp.bfloat16


class Exchange:
    def __init__(self, group, src, land, whole, send, recv):
        self.steps, self.me, self.peer, self.dev = group
        self.src, self.land, self.whole, self.send, self.recv = src, land, whole, send, recv

    def start(self):
        @pl.loop(0, self.steps)
        def _(i):
            to = self.peer(i)
            pltpu.make_async_remote_copy(
                src_ref=self.src(to),
                dst_ref=self.land(self.me),
                send_sem=self.send,
                recv_sem=self.recv,
                device_id=self.dev(to),
                device_id_type=MESH,
            ).start()

    def _all(self):
        part = self.whole.at[pl.ds(0, self.steps)]
        return pltpu.make_async_remote_copy(
            src_ref=part,
            dst_ref=part,
            send_sem=self.send,
            recv_sem=self.recv,
            device_id=self.dev(self.peer(0)),
            device_id_type=MESH,
        )

    def wait(self):
        self._all().wait_recv()

    def finish(self):
        self._all().wait_send()


def ring(n, me, dev, far_first):
    def offset(i):
        if not far_first:
            return i + 1
        return n // 2 + (1 - 2 * (i % 2)) * ((i + 1) // 2)

    return (
        n - 1,
        me,
        lambda i: lax.rem(me + offset(i), n),
        dev,
    )


def plane(nr, q, r, dev):
    y_lo, core, y_hi, x = q // 2, lax.rem(q, 2), r // 4, lax.rem(r, 4)
    n = NQ * nr

    def member(i):
        t = n - 1 - i
        b = (t // 4) % 4
        dx = (3 * b + 3 * (b // 2) - 2 * (b // 3)) % 4
        to_x = lax.rem(x + dx, 4)
        to_hi = lax.rem(y_hi + t // 16, 2)
        to_lo = lax.rem(y_lo + (t // 2) % 2, 2)
        to_core = lax.rem(core + t % 2, 2)
        return (to_lo * 2 + to_core) * nr + to_hi * 4 + to_x

    return (n - 1, q * nr + r, member, dev)


def to_tiles(x):
    y = x.reshape(8, 8, 256)
    return jnp.stack([y[..., :128], y[..., 128:]], axis=1).reshape(16, 8, 128)


def from_tiles(x):
    y = x.reshape(8, 2, 8, 128)
    return jnp.concatenate([y[:, 0], y[:, 1]], axis=-1).reshape(64, 256)


def join_shares(x):
    y = x.reshape(16, 2, 4, 128)
    return from_tiles(jnp.concatenate([y[:, 0], y[:, 1]], axis=1))


def kernel(
    nz, nr, user_step, item_step, grad_scale,
    blocks, row_hbm, col_hbm, ctx_hbm, live_hbm, user_hbm, item_hbm, factor_hbm,
    new_users, new_items, ctx_out,
    xb, gu, idx, bmat, amat, iq, ist, zg, ys, rg, vf, wf, ub, user_t, item_t, ctx_t,
    xs0, xr0, xs1, xr1, us, ur, zs, zr, cz, fs, fin,
    row_of, col_of, ctx_of, live_of, user_in, item_in, ctx_in, insem,
    xsem, rsend, rrecv, qsend, qrecv, zsend, zrecv, psend, precv,
):
    blk = lax.axis_index("blk")
    r = lax.axis_index("rows")
    z, q = blk // NQ, lax.rem(blk, NQ)
    me = q * nr + r
    slots = xb.shape[0]
    members = NQ * nr
    groups = {
        "r": ring(nr, r, lambda i: (blk, i), False),
        "q": ring(NQ, q, lambda i: (z * NQ + i, r), False),
        "z": ring(nz, z, lambda i: (i * NQ + q, r), True),
        "p": plane(nr, q, r, lambda i: (z * NQ + i // nr, lax.rem(i, nr))),
    }
    semaphores = {
        "r": (rsend, rrecv), "q": (qsend, qrecv), "z": (zsend, zrecv), "p": (psend, precv),
    }

    pending = []
    used = {"r": 0, "q": 0, "z": 0, "p": 0}

    def exchange(kind, src, land, whole):
        send, recv = semaphores[kind]
        at = used[kind]
        used[kind] += 1
        e = Exchange(groups[kind], src, land, whole, send.at[at], recv.at[at])
        e.start()
        pending.append(e)
        return e

    barrier = pltpu.get_barrier_semaphore()
    for kind in ("z", "p"):
        steps, _, peer, dev = groups[kind]

        @pl.loop(0, steps)
        def _(i):
            pl.semaphore_signal(
                barrier, inc=1, device_id=dev(peer(i)), device_id_type=MESH
            )

    inputs = [
        pltpu.make_async_copy(src, dst, insem.at[i])
        for i, (src, dst) in enumerate(
            (
                (item_hbm, item_in),
                (live_hbm, live_of),
                (col_hbm, col_of),
                (user_hbm, user_in),
                (row_hbm, row_of),
                (ctx_hbm, ctx_of),
                (factor_hbm, ctx_in),
            )
        )
    ]
    for c in inputs:
        c.start()
    load = pltpu.make_async_copy(blocks.at[0, 0], xb, xsem)
    load.start()
    for c in inputs:
        c.wait()
    live = live_of[0, 0]
    rows = [row_of[0, 0, s] for s in range(slots)]
    ctxs = [ctx_of[0, 0, s] for s in range(slots)]
    alive = [(s < live).astype(jnp.int32) for s in range(slots)]

    item_tiles = to_tiles(item_in[...])
    halves = [item_tiles, jnp.concatenate([item_tiles[:, 4:], item_tiles[:, :4]], axis=1)]
    ist[...] = jnp.stack(halves, axis=1).reshape(members, 8, 128)
    iq[q] = ist[me]
    sub = lax.broadcasted_iota(jnp.int32, (8, 128), 0)
    start = jnp.full((8, 128), -1000, jnp.int32)
    for s in range(slots):
        at = (col_of[0, 0, s] * 4) * alive[s] - 1000 * (1 - alive[s])
        start = jnp.where(sub == s, at, start)
    idx[me] = start
    user_own = user_in[...]
    gu[0, r] = user_own.astype(BF16)

    pl.semaphore_wait(barrier, nz - 1 + members - 1)

    item_first = exchange("q", lambda i: ist.at[i * nr + r], lambda i: iq.at[i], iq)
    index_gather = exchange("p", lambda i: idx.at[me], lambda i: idx.at[i], idx)
    item_first.wait()
    item_own = jnp.concatenate([iq[i][:4] for i in range(NQ)], axis=0)
    item_delta = jnp.zeros((16, 128), F32)
    zg[0, z] = item_own.astype(BF16)

    for k in range(ITERS):
        last = k == ITERS - 1
        z_gather = exchange("z", lambda i, k=k: zg.at[k, z], lambda i, k=k: zg.at[k, i], zg.at[k])
        if k == 0:
            user_gather = exchange("r", lambda i: gu.at[0, r], lambda i: gu.at[0, i], gu.at[0])
            for s in range(slots):
                w = ctx_in[...].astype(BF16).astype(F32)
                second = ctxs[s].astype(F32)
                wf[s] = w[:64] * (1.0 - second) + w[64:] * second
            index_gather.wait()
            sub3 = lax.broadcasted_iota(jnp.int32, (members, 8, 128), 1)
            row = [
                jnp.broadcast_to(idx[:, pl.ds(s, 1), :], (members, 8, 128)) for s in range(slots)
            ]
            first = jnp.where(sub3 < 4, row[0], row[1]) + lax.rem(sub3, 4)
            second = jnp.where(sub3 < 4, row[2], -1000) + lax.rem(sub3, 4)
            count = members * 16
            wanted = jnp.concatenate([first, second], axis=1).reshape(count, 128)
            total_rows = nz * 16
            lane = lax.broadcasted_iota(jnp.int32, (count, 128), 1)
            for c in range(total_rows // 128):
                hit = jnp.where(lane + 128 * c == wanted, 1.0, 0.0)
                bmat[:, 128 * c : 128 * (c + 1)] = hit.astype(BF16)
            at_row = lax.broadcasted_iota(jnp.int32, (total_rows, 128), 0)
            i0 = lax.broadcasted_iota(jnp.int32, (128, 128), 0)
            i1 = lax.broadcasted_iota(jnp.int32, (128, 128), 1)
            for c in range(count // 128):
                part = jnp.where(i0 == i1, wanted[128 * c : 128 * (c + 1)], 0)
                along = jnp.sum(part, axis=0, keepdims=True)
                hit = jnp.where(at_row == along, 1.0, 0.0)
                amat[:, 128 * c : 128 * (c + 1)] = hit.astype(BF16)
        z_gather.wait()
        shares = zg[k].reshape(nz * 16, 128)
        picked = jnp.dot(bmat[...], shares, preferred_element_type=F32)
        ys[k] = picked.astype(BF16).reshape(members, 16, 128)
        rg[k, me] = ys[k, me]
        answer = exchange("p", lambda i, k=k: ys.at[k, i], lambda i, k=k: rg.at[k, i], rg.at[k])
        user_gather.wait()
        for s in range(slots):
            total = jnp.zeros((64, 256), F32)
            for p in range(nr):
                total += gu[k, p].astype(F32) * (rows[s] == p).astype(jnp.int32).astype(F32)
            ub[s] = total.astype(BF16)
        user_t[...] = jnp.zeros_like(user_t)
        if last:
            ctx_t[...] = jnp.zeros_like(ctx_t)
        else:
            load.wait()
        answer.wait()
        got = rg[k].astype(F32)
        for s in range(slots):
            vf[s] = join_shares(got[:, 4 * s : 4 * s + 4, :])

        @pl.loop(0, 8)
        def _(c):
            for s in range(slots):
                u, w = ub[s], wf[s]
                v = vf[s, pl.ds(pl.multiple_of(c * 8, 8), 8), :]
                pair = (v[:, None, :] * w[None, :, :]).astype(BF16).reshape(512, 256)
                model = lax.dot_general(
                    u, pair, (((1,), (1,)), ((), ())), preferred_element_type=F32
                )
                x = xb[s, :, pl.ds(pl.multiple_of(c * 512, 512), 512)]
                resid = (model - x.astype(F32)).astype(BF16)
                user_t[s] += jnp.dot(resid, pair, preferred_element_type=F32)
                g = lax.dot_general(
                    resid, u, (((0,), (0,)), ((), ())), preferred_element_type=F32
                ).reshape(8, 64, 256)
                item_t[s, pl.ds(pl.multiple_of(c * 8, 8), 8), :] = jnp.sum(g * w[None], axis=1)
                if last:
                    ctx_t[s] += jnp.sum(g * v[:, None, :], axis=0)

        xs, xr = (xs1, xr1) if last else (xs0, xr0)
        tiles = [to_tiles(item_t[s]) for s in range(slots)]
        fill = jnp.zeros((16, 4, 128), F32)
        for half in range(2):
            cut = [t[:, 4 * half : 4 * half + 4] for t in tiles]
            part = jnp.concatenate(cut + [fill], axis=1).astype(BF16)
            for v in range(16):
                xs[2 * v + half, pl.ds(0, 16), :] = part[v]
        if last:
            for c in range(2):
                total = jnp.zeros((64, 256), F32)
                for s in range(slots):
                    mine = alive[s] * (ctxs[s] == c).astype(jnp.int32)
                    total += ctx_t[s] * mine.astype(F32)
                part = to_tiles(total)
                part = jnp.concatenate([part, jnp.zeros_like(part)], axis=1).astype(BF16)
                xs[pl.ds(16 * c, 16), pl.ds(16, 16), :] = part
        xr[me] = xs[me]
        item_parts = exchange("p", lambda i, xs=xs: xs.at[i], lambda i, xr=xr: xr.at[i], xr)
        for p in range(nr):
            total = jnp.zeros((64, 256), F32)
            for s in range(slots):
                mine = alive[s] * (rows[s] == p).astype(jnp.int32)
                total += user_t[s] * mine.astype(F32)
            us[k, p] = total.astype(BF16)
        ur[k, r] = us[k, r]
        user_parts = exchange("r", lambda i, k=k: us.at[k, i], lambda i, k=k: ur.at[k, i], ur.at[k])

        item_parts.wait()
        parts = xr[:, :16, :].reshape(members * 16, 128)
        summed = jnp.dot(amat[...], parts, preferred_element_type=F32)
        zs[k] = summed.astype(BF16).reshape(nz, 16, 128)
        zr[k, z] = zs[k, z]
        z_parts = exchange("z", lambda i, k=k: zs.at[k, i], lambda i, k=k: zr.at[k, i], zr.at[k])
        if last:
            cz[z] = jnp.sum(xr[:, 16:, :].astype(F32), axis=0)[:8]
            ctx_z = exchange("z", lambda i: cz.at[z], lambda i: cz.at[i], cz)
        user_parts.wait()
        user_own = user_own - user_step * jnp.sum(ur[k].astype(F32), axis=0)
        if last:
            new_users[...] = user_own
        else:
            gu[k + 1, r] = user_own.astype(BF16)
            user_gather = exchange(
                "r", lambda i, k=k: gu.at[k + 1, r], lambda i, k=k: gu.at[k + 1, i], gu.at[k + 1])
        z_parts.wait()
        item_delta = item_delta + item_step * jnp.sum(zr[k].astype(F32), axis=0)
        if not last:
            zg[k + 1, z] = (item_own - item_delta).astype(BF16)

    ctx_z.wait()
    ctx_share = jnp.sum(cz[...], axis=0) * grad_scale
    for i in range(NQ):
        part = item_delta[4 * i : 4 * i + 4]
        rest = part - part.astype(BF16).astype(F32)
        fs[i] = jnp.concatenate([part, rest, ctx_share], axis=0).astype(BF16)
    fin[me] = fs[q]
    final = exchange("p", lambda i: fs.at[i // nr], lambda i: fin.at[i], fin)
    final.wait()
    got = fin[...].astype(F32)
    new_items[...] = item_in[...] - join_shares(got[:, :4] + got[:, 4:8])
    for c in range(2):
        ctx_out[pl.ds(64 * c, 64), :] = from_tiles(got[16 * c : 16 * c + 16, 8:])
    for e in pending:
        e.finish()


def local(
    blocks, block_row, block_col, block_ctx, live_blocks, user_factor, item_factor, context_factor
):
    nr = lax.axis_size("rows")
    nz = lax.axis_size("blk") // NQ
    slots = blocks.shape[2]
    nb = nz * NQ
    edge = blocks.shape[3]
    vm = pltpu.VMEM
    dma = pltpu.SemaphoreType.DMA
    members = NQ * nr
    scratch = [
        vm((slots, 64, 4096), BF16),
        vm((ITERS, nr, 64, 256), BF16),
        vm((members, 8, 128), jnp.int32),
        vm((members * 16, nz * 16), BF16),
        vm((nz * 16, members * 16), BF16),
        vm((NQ, 8, 128), F32),
        vm((members, 8, 128), F32),
        vm((ITERS, nz, 16, 128), BF16),
        vm((ITERS, members, 16, 128), BF16),
        vm((ITERS, members, 16, 128), BF16),
        vm((slots, 64, 256), F32),
        vm((slots, 64, 256), F32),
        vm((slots, 64, 256), BF16),
        vm((slots, 64, 256), F32),
        vm((slots, 64, 256), F32),
        vm((slots, 64, 256), F32),
        vm((members, 16, 128), BF16),
        vm((members, 16, 128), BF16),
        vm((members, 32, 128), BF16),
        vm((members, 32, 128), BF16),
        vm((ITERS, nr, 64, 256), BF16),
        vm((ITERS, nr, 64, 256), BF16),
        vm((ITERS, nz, 16, 128), BF16),
        vm((ITERS, nz, 16, 128), BF16),
        vm((nz, 8, 128), F32),
        vm((NQ, 16, 128), BF16),
        vm((members, 16, 128), BF16),
        pltpu.SMEM((1, 1, slots), jnp.int32),
        pltpu.SMEM((1, 1, slots), jnp.int32),
        pltpu.SMEM((1, 1, slots), jnp.int32),
        pltpu.SMEM((1, 1), jnp.int32),
        vm((64, 256), F32),
        vm((64, 256), F32),
        vm((128, 256), F32),
        dma((7,)),
        dma,
        dma((4,)),
        dma((4,)),
        dma((1,)),
        dma((1,)),
        dma((5,)),
        dma((5,)),
        dma((6,)),
        dma((6,)),
    ]
    body = functools.partial(
        kernel,
        nz,
        nr,
        6.4 / (edge * edge),
        16.0 / (edge * edge * nr),
        8.0 / (edge * math.sqrt(nb * nr)),
    )
    in_vmem = pl.BlockSpec(memory_space=pltpu.VMEM)
    return pl.pallas_call(
        body,
        out_shape=(
            jax.ShapeDtypeStruct(user_factor.shape, F32),
            jax.ShapeDtypeStruct(item_factor.shape, F32),
            jax.ShapeDtypeStruct(context_factor.shape, F32),
        ),
        in_specs=[pl.BlockSpec(memory_space=pltpu.HBM)] * 8,
        out_specs=(in_vmem,) * 3,
        scratch_shapes=scratch,
        compiler_params=pltpu.CompilerParams(
            collective_id=0, has_side_effects=True, vmem_limit_bytes=56 * 1024 * 1024
        ),
    )(
        blocks, block_row, block_col, block_ctx, live_blocks,
        user_factor, item_factor, context_factor,
    )


def solution(mesh):
    return jax.shard_map(
        local,
        mesh=mesh,
        in_specs=(
            P("blk", "rows", None, None, None),
            P("blk", "rows", None),
            P("blk", "rows", None),
            P("blk", "rows", None),
            P("blk", "rows"),
            P(("blk", "rows"), None),
            P("blk", None),
            P(),
        ),
        out_specs=(P(("blk", "rows"), None), P("blk", None), P()),
        check_vma=False,
    )
```

```python
import functools
import math

import jax
import jax.numpy as jnp
from jax import lax
from jax.experimental import pallas as pl
from jax.experimental.pallas import tpu as pltpu
from jax.sharding import PartitionSpec as P

ITERS = 2
NQ = 4
MESH = pl.DeviceIdType.MESH
F32 = jnp.float32
BF16 = jnp.bfloat16


class Exchange:
    def __init__(self, group, src, land, whole, send, recv):
        self.steps, self.me, self.peer, self.dev = group
        self.src, self.land, self.whole, self.send, self.recv = src, land, whole, send, recv

    def start(self):
        for i in range(self.steps):
            to = self.peer(i)
            pltpu.make_async_remote_copy(
                src_ref=self.src(to),
                dst_ref=self.land(self.me),
                send_sem=self.send,
                recv_sem=self.recv,
                device_id=self.dev(to),
                device_id_type=MESH,
            ).start()

    def _all(self):
        part = self.whole.at[pl.ds(0, self.steps)]
        return pltpu.make_async_remote_copy(
            src_ref=part,
            dst_ref=part,
            send_sem=self.send,
            recv_sem=self.recv,
            device_id=self.dev(self.peer(0)),
            device_id_type=MESH,
        )

    def wait(self):
        self._all().wait_recv()

    def finish(self):
        self._all().wait_send()


def ring(n, me, dev, far_first):
    def offset(i):
        if not far_first:
            return i + 1
        return n // 2 + (1 - 2 * (i % 2)) * ((i + 1) // 2)

    return (
        n - 1,
        me,
        lambda i: lax.rem(me + offset(i), n),
        dev,
    )


def plane(nr, q, r, dev):
    y_lo, core, y_hi, x = q // 2, lax.rem(q, 2), r // 4, lax.rem(r, 4)
    n = NQ * nr

    xs = [lax.rem(x + d, 4) for d in range(4)]
    his = [y_hi * 4, (1 - y_hi) * 4]
    qs = [
        (lo * 2 + c) * nr for lo in (y_lo, 1 - y_lo) for c in (core, 1 - core)
    ]
    rows = [hi + xx for hi in his for xx in xs]
    hops = [(dhi * 2 if not dlo else 1) + min(d, 4 - d) + dlo * (1 - dhi)
            for dlo in range(2) for dhi in range(2) for d in range(4)]
    order = sorted(
        (-hops[(dlo * 2 + dhi) * 4 + d], dlo * 2 + c, dhi * 4 + d)
        for dlo in range(2) for c in range(2) for dhi in range(2) for d in range(4)
    )
    steps = [(a, b) for _, a, b in order if (a, b) != (0, 0)]

    def member(i):
        a, b = steps[i]
        return qs[a] + rows[b]

    return (n - 1, q * nr + r, member, dev)


def to_tiles(x):
    y = x.reshape(8, 8, 256)
    return jnp.stack([y[..., :128], y[..., 128:]], axis=1).reshape(16, 8, 128)


def from_tiles(x):
    y = x.reshape(8, 2, 8, 128)
    return jnp.concatenate([y[:, 0], y[:, 1]], axis=-1).reshape(64, 256)


def join_shares(x):
    y = x.reshape(16, 2, 4, 128)
    return from_tiles(jnp.concatenate([y[:, 0], y[:, 1]], axis=1))


def kernel(
    nz, nr, user_step, item_step, grad_scale,
    blocks, row_hbm, col_hbm, ctx_hbm, live_hbm, user_hbm, item_hbm, factor_hbm,
    new_users, new_items, ctx_out,
    xb, gu, idx, bmat, amat, iq, ist, zg, ys, rg, vf, wf, ub, user_t, item_t, ctx_t,
    xs0, xr0, xs1, xr1, us, ur, zs, zr, cz, fs, fin,
    row_of, col_of, ctx_of, live_of, user_in, item_in, ctx_in, insem,
    xsem, rsend, rrecv, qsend, qrecv, zsend, zrecv, psend, precv,
):
    blk = lax.axis_index("blk")
    r = lax.axis_index("rows")
    z, q = blk // NQ, lax.rem(blk, NQ)
    me = q * nr + r
    slots = xb.shape[0]
    members = NQ * nr
    groups = {
        "r": ring(nr, r, lambda i: (blk, i), False),
        "q": ring(NQ, q, lambda i: (z * NQ + i, r), False),
        "z": ring(nz, z, lambda i: (i * NQ + q, r), True),
        "p": plane(nr, q, r, lambda i: (z * NQ + i // nr, lax.rem(i, nr))),
    }
    semaphores = {
        "r": (rsend, rrecv), "q": (qsend, qrecv), "z": (zsend, zrecv), "p": (psend, precv),
    }

    pending = []
    used = {"r": 0, "q": 0, "z": 0, "p": 0}

    def exchange(kind, src, land, whole):
        send, recv = semaphores[kind]
        at = used[kind]
        used[kind] += 1
        e = Exchange(groups[kind], src, land, whole, send.at[at], recv.at[at])
        e.start()
        pending.append(e)
        return e

    barrier = pltpu.get_barrier_semaphore()
    for kind in ("z", "p"):
        steps, _, peer, dev = groups[kind]

        for i in range(steps):
            pl.semaphore_signal(
                barrier, inc=1, device_id=dev(peer(i)), device_id_type=MESH
            )

    inputs = [
        pltpu.make_async_copy(src, dst, insem.at[i])
        for i, (src, dst) in enumerate(
            (
                (item_hbm, item_in),
                (live_hbm, live_of),
                (col_hbm, col_of),
                (user_hbm, user_in),
                (row_hbm, row_of),
                (ctx_hbm, ctx_of),
                (factor_hbm, ctx_in),
            )
        )
    ]
    for c in inputs:
        c.start()
    load = pltpu.make_async_copy(blocks.at[0, 0], xb, xsem)
    load.start()
    for c in inputs:
        c.wait()
    live = live_of[0, 0]
    rows = [row_of[0, 0, s] for s in range(slots)]
    ctxs = [ctx_of[0, 0, s] for s in range(slots)]
    alive = [(s < live).astype(jnp.int32) for s in range(slots)]

    item_tiles = to_tiles(item_in[...])
    halves = [item_tiles, jnp.concatenate([item_tiles[:, 4:], item_tiles[:, :4]], axis=1)]
    ist[...] = jnp.stack(halves, axis=1).reshape(members, 8, 128)
    iq[q] = ist[me]
    sub = lax.broadcasted_iota(jnp.int32, (8, 128), 0)
    start = jnp.full((8, 128), -1000, jnp.int32)
    for s in range(slots):
        at = (col_of[0, 0, s] * 4) * alive[s] - 1000 * (1 - alive[s])
        start = jnp.where(sub == s, at, start)
    idx[me] = start
    user_own = user_in[...]
    gu[0, r] = user_own.astype(BF16)

    pl.semaphore_wait(barrier, nz - 1 + members - 1)

    item_first = exchange("q", lambda i: ist.at[i * nr + r], lambda i: iq.at[i], iq)
    index_gather = exchange("p", lambda i: idx.at[me], lambda i: idx.at[i], idx)
    item_first.wait()
    item_own = jnp.concatenate([iq[i][:4] for i in range(NQ)], axis=0)
    item_delta = jnp.zeros((16, 128), F32)
    zg[0, z] = item_own.astype(BF16)

    for k in range(ITERS):
        last = k == ITERS - 1
        z_gather = exchange("z", lambda i, k=k: zg.at[k, z], lambda i, k=k: zg.at[k, i], zg.at[k])
        if k == 0:
            user_gather = exchange("r", lambda i: gu.at[0, r], lambda i: gu.at[0, i], gu.at[0])
            for s in range(slots):
                w = ctx_in[...].astype(BF16).astype(F32)
                second = ctxs[s].astype(F32)
                wf[s] = w[:64] * (1.0 - second) + w[64:] * second
            index_gather.wait()
            sub3 = lax.broadcasted_iota(jnp.int32, (members, 8, 128), 1)
            row = [
                jnp.broadcast_to(idx[:, pl.ds(s, 1), :], (members, 8, 128)) for s in range(slots)
            ]
            first = jnp.where(sub3 < 4, row[0], row[1]) + lax.rem(sub3, 4)
            second = jnp.where(sub3 < 4, row[2], -1000) + lax.rem(sub3, 4)
            count = members * 16
            wanted = jnp.concatenate([first, second], axis=1).reshape(count, 128)
            total_rows = nz * 16
            lane = lax.broadcasted_iota(jnp.int32, (count, 128), 1)
            for c in range(total_rows // 128):
                hit = jnp.where(lane + 128 * c == wanted, 1.0, 0.0)
                bmat[:, 128 * c : 128 * (c + 1)] = hit.astype(BF16)
            at_row = lax.broadcasted_iota(jnp.int32, (total_rows, 128), 0)
            i0 = lax.broadcasted_iota(jnp.int32, (128, 128), 0)
            i1 = lax.broadcasted_iota(jnp.int32, (128, 128), 1)
            for c in range(count // 128):
                part = jnp.where(i0 == i1, wanted[128 * c : 128 * (c + 1)], 0)
                along = jnp.sum(part, axis=0, keepdims=True)
                hit = jnp.where(at_row == along, 1.0, 0.0)
                amat[:, 128 * c : 128 * (c + 1)] = hit.astype(BF16)
        z_gather.wait()
        shares = zg[k].reshape(nz * 16, 128)
        picked = jnp.dot(bmat[...], shares, preferred_element_type=F32)
        ys[k] = picked.astype(BF16).reshape(members, 16, 128)
        rg[k, me] = ys[k, me]
        answer = exchange("p", lambda i, k=k: ys.at[k, i], lambda i, k=k: rg.at[k, i], rg.at[k])
        user_gather.wait()
        for s in range(slots):
            total = jnp.zeros((64, 256), F32)
            for p in range(nr):
                total += gu[k, p].astype(F32) * (rows[s] == p).astype(jnp.int32).astype(F32)
            ub[s] = total.astype(BF16)
        user_t[...] = jnp.zeros_like(user_t)
        if last:
            ctx_t[...] = jnp.zeros_like(ctx_t)
        else:
            load.wait()
        answer.wait()
        got = rg[k].astype(F32)
        for s in range(slots):
            vf[s] = join_shares(got[:, 4 * s : 4 * s + 4, :])

        @pl.loop(0, 2)
        def _(c):
            for s in range(slots):
                u, w = ub[s], wf[s]
                v = vf[s, pl.ds(pl.multiple_of(c * 32, 32), 32), :]
                pair = (v[:, None, :] * w[None, :, :]).astype(BF16).reshape(2048, 256)
                model = lax.dot_general(
                    u, pair, (((1,), (1,)), ((), ())), preferred_element_type=F32
                )
                x = xb[s, :, pl.ds(pl.multiple_of(c * 2048, 2048), 2048)]
                resid = (model - x.astype(F32)).astype(BF16)
                user_t[s] += jnp.dot(resid, pair, preferred_element_type=F32)
                g = lax.dot_general(
                    resid, u, (((0,), (0,)), ((), ())), preferred_element_type=F32
                ).reshape(32, 64, 256)
                item_t[s, pl.ds(pl.multiple_of(c * 32, 32), 32), :] = jnp.sum(g * w[None], axis=1)
                if last:
                    ctx_t[s] += jnp.sum(g * v[:, None, :], axis=0)

        xs, xr = (xs1, xr1) if last else (xs0, xr0)
        tiles = [to_tiles(item_t[s]) for s in range(slots)]
        fill = jnp.zeros((16, 4, 128), F32)
        for half in range(2):
            cut = [t[:, 4 * half : 4 * half + 4] for t in tiles]
            part = jnp.concatenate(cut + [fill], axis=1).astype(BF16)
            for v in range(16):
                xs[2 * v + half, pl.ds(0, 16), :] = part[v]
        if last:
            for c in range(2):
                total = jnp.zeros((64, 256), F32)
                for s in range(slots):
                    mine = alive[s] * (ctxs[s] == c).astype(jnp.int32)
                    total += ctx_t[s] * mine.astype(F32)
                part = to_tiles(total)
                part = jnp.concatenate([part, jnp.zeros_like(part)], axis=1).astype(BF16)
                xs[pl.ds(16 * c, 16), pl.ds(16, 16), :] = part
        xr[me] = xs[me]
        item_parts = exchange("p", lambda i, xs=xs: xs.at[i], lambda i, xr=xr: xr.at[i], xr)
        for p in range(nr):
            total = jnp.zeros((64, 256), F32)
            for s in range(slots):
                mine = alive[s] * (rows[s] == p).astype(jnp.int32)
                total += user_t[s] * mine.astype(F32)
            us[k, p] = total.astype(BF16)
        ur[k, r] = us[k, r]
        user_parts = exchange("r", lambda i, k=k: us.at[k, i], lambda i, k=k: ur.at[k, i], ur.at[k])

        item_parts.wait()
        parts = xr[:, :16, :].reshape(members * 16, 128)
        summed = jnp.dot(amat[...], parts, preferred_element_type=F32)
        zs[k] = summed.astype(BF16).reshape(nz, 16, 128)
        zr[k, z] = zs[k, z]
        z_parts = exchange("z", lambda i, k=k: zs.at[k, i], lambda i, k=k: zr.at[k, i], zr.at[k])
        if last:
            cz[z] = jnp.sum(xr[:, 16:, :].astype(F32), axis=0)[:8]
            ctx_z = exchange("z", lambda i: cz.at[z], lambda i: cz.at[i], cz)
        user_parts.wait()
        user_own = user_own - user_step * jnp.sum(ur[k].astype(F32), axis=0)
        if last:
            new_users[...] = user_own
        else:
            gu[k + 1, r] = user_own.astype(BF16)
            user_gather = exchange(
                "r", lambda i, k=k: gu.at[k + 1, r], lambda i, k=k: gu.at[k + 1, i], gu.at[k + 1])
        z_parts.wait()
        item_delta = item_delta + item_step * jnp.sum(zr[k].astype(F32), axis=0)
        if not last:
            zg[k + 1, z] = (item_own - item_delta).astype(BF16)

    ctx_z.wait()
    ctx_share = jnp.sum(cz[...], axis=0) * grad_scale
    for i in range(NQ):
        part = item_delta[4 * i : 4 * i + 4]
        rest = part - part.astype(BF16).astype(F32)
        fs[i] = jnp.concatenate([part, rest, ctx_share], axis=0).astype(BF16)
    fin[me] = fs[q]
    final = exchange("p", lambda i: fs.at[i // nr], lambda i: fin.at[i], fin)
    final.wait()
    got = fin[...].astype(F32)
    new_items[...] = item_in[...] - join_shares(got[:, :4] + got[:, 4:8])
    for c in range(2):
        ctx_out[pl.ds(64 * c, 64), :] = from_tiles(got[16 * c : 16 * c + 16, 8:])
    for e in pending:
        e.finish()


def local(
    blocks, block_row, block_col, block_ctx, live_blocks, user_factor, item_factor, context_factor
):
    nr = lax.axis_size("rows")
    nz = lax.axis_size("blk") // NQ
    slots = blocks.shape[2]
    nb = nz * NQ
    edge = blocks.shape[3]
    vm = pltpu.VMEM
    dma = pltpu.SemaphoreType.DMA
    members = NQ * nr
    scratch = [
        vm((slots, 64, 4096), BF16),
        vm((ITERS, nr, 64, 256), BF16),
        vm((members, 8, 128), jnp.int32),
        vm((members * 16, nz * 16), BF16),
        vm((nz * 16, members * 16), BF16),
        vm((NQ, 8, 128), F32),
        vm((members, 8, 128), F32),
        vm((ITERS, nz, 16, 128), BF16),
        vm((ITERS, members, 16, 128), BF16),
        vm((ITERS, members, 16, 128), BF16),
        vm((slots, 64, 256), F32),
        vm((slots, 64, 256), F32),
        vm((slots, 64, 256), BF16),
        vm((slots, 64, 256), F32),
        vm((slots, 64, 256), F32),
        vm((slots, 64, 256), F32),
        vm((members, 16, 128), BF16),
        vm((members, 16, 128), BF16),
        vm((members, 32, 128), BF16),
        vm((members, 32, 128), BF16),
        vm((ITERS, nr, 64, 256), BF16),
        vm((ITERS, nr, 64, 256), BF16),
        vm((ITERS, nz, 16, 128), BF16),
        vm((ITERS, nz, 16, 128), BF16),
        vm((nz, 8, 128), F32),
        vm((NQ, 16, 128), BF16),
        vm((members, 16, 128), BF16),
        pltpu.SMEM((1, 1, slots), jnp.int32),
        pltpu.SMEM((1, 1, slots), jnp.int32),
        pltpu.SMEM((1, 1, slots), jnp.int32),
        pltpu.SMEM((1, 1), jnp.int32),
        vm((64, 256), F32),
        vm((64, 256), F32),
        vm((128, 256), F32),
        dma((7,)),
        dma,
        dma((4,)),
        dma((4,)),
        dma((1,)),
        dma((1,)),
        dma((5,)),
        dma((5,)),
        dma((6,)),
        dma((6,)),
    ]
    body = functools.partial(
        kernel,
        nz,
        nr,
        6.4 / (edge * edge),
        16.0 / (edge * edge * nr),
        8.0 / (edge * math.sqrt(nb * nr)),
    )
    in_vmem = pl.BlockSpec(memory_space=pltpu.VMEM)
    return pl.pallas_call(
        body,
        out_shape=(
            jax.ShapeDtypeStruct(user_factor.shape, F32),
            jax.ShapeDtypeStruct(item_factor.shape, F32),
            jax.ShapeDtypeStruct(context_factor.shape, F32),
        ),
        in_specs=[pl.BlockSpec(memory_space=pltpu.HBM)] * 8,
        out_specs=(in_vmem,) * 3,
        scratch_shapes=scratch,
        compiler_params=pltpu.CompilerParams(
            collective_id=0, has_side_effects=True, vmem_limit_bytes=56 * 1024 * 1024
        ),
    )(
        blocks, block_row, block_col, block_ctx, live_blocks,
        user_factor, item_factor, context_factor,
    )


def solution(mesh):
    return jax.shard_map(
        local,
        mesh=mesh,
        in_specs=(
            P("blk", "rows", None, None, None),
            P("blk", "rows", None),
            P("blk", "rows", None),
            P("blk", "rows", None),
            P("blk", "rows"),
            P(("blk", "rows"), None),
            P("blk", None),
            P(),
        ),
        out_specs=(P(("blk", "rows"), None), P("blk", None), P()),
        check_vma=False,
    )
```

```python
import functools
import math

import jax
import jax.numpy as jnp
from jax import lax
from jax.experimental import pallas as pl
from jax.experimental.pallas import tpu as pltpu
from jax.sharding import PartitionSpec as P

ITERS = 2
NQ = 4
MESH = pl.DeviceIdType.MESH
F32 = jnp.float32
BF16 = jnp.bfloat16


class Exchange:
    def __init__(self, group, src, land, whole, send, recv):
        self.steps, self.me, self.peer, self.dev = group
        self.src, self.land, self.whole, self.send, self.recv = src, land, whole, send, recv

    def start(self):
        for i in range(self.steps):
            to = self.peer(i)
            pltpu.make_async_remote_copy(
                src_ref=self.src(to),
                dst_ref=self.land(self.me),
                send_sem=self.send,
                recv_sem=self.recv,
                device_id=self.dev(to),
                device_id_type=MESH,
            ).start()

    def _all(self):
        part = self.whole.at[pl.ds(0, self.steps)]
        return pltpu.make_async_remote_copy(
            src_ref=part,
            dst_ref=part,
            send_sem=self.send,
            recv_sem=self.recv,
            device_id=self.dev(self.peer(0)),
            device_id_type=MESH,
        )

    def wait(self):
        self._all().wait_recv()

    def finish(self):
        self._all().wait_send()


def ring(n, me, dev, far_first):
    def offset(i):
        if not far_first:
            return i + 1
        return n // 2 + (1 - 2 * (i % 2)) * ((i + 1) // 2)

    return (
        n - 1,
        me,
        lambda i: lax.rem(me + offset(i), n),
        dev,
    )


def plane(nr, q, r, dev):
    y_lo, core, y_hi, x = q // 2, lax.rem(q, 2), r // 4, lax.rem(r, 4)
    n = NQ * nr

    xs = [lax.rem(x + d, 4) for d in range(4)]
    his = [y_hi * 4, (1 - y_hi) * 4]
    qs = [
        (lo * 2 + c) * nr for lo in (y_lo, 1 - y_lo) for c in (core, 1 - core)
    ]
    rows = [hi + xx for hi in his for xx in xs]
    hops = [(dhi * 2 if not dlo else 1) + min(d, 4 - d) + dlo * (1 - dhi)
            for dlo in range(2) for dhi in range(2) for d in range(4)]
    order = sorted(
        (-hops[(dlo * 2 + dhi) * 4 + d], dlo * 2 + c, dhi * 4 + d)
        for dlo in range(2) for c in range(2) for dhi in range(2) for d in range(4)
    )
    steps = [(a, b) for _, a, b in order if (a, b) != (0, 0)]

    def member(i):
        a, b = steps[i]
        return qs[a] + rows[b]

    return (n - 1, q * nr + r, member, dev)


def to_tiles(x):
    y = x.reshape(8, 8, 256)
    return jnp.stack([y[..., :128], y[..., 128:]], axis=1).reshape(16, 8, 128)


def from_tiles(x):
    y = x.reshape(8, 2, 8, 128)
    return jnp.concatenate([y[:, 0], y[:, 1]], axis=-1).reshape(64, 256)


def join_shares(x):
    y = x.reshape(16, 2, 4, 128)
    return from_tiles(jnp.concatenate([y[:, 0], y[:, 1]], axis=1))


def kernel(
    nz, nr, user_step, item_step, grad_scale,
    blocks, row_hbm, col_hbm, ctx_hbm, live_hbm, user_hbm, item_hbm, factor_hbm,
    new_users, new_items, ctx_out,
    xb, gu, idx, bmat, amat, iq, ist, zg, ys, rg, vf, wf, ub, user_t, item_t, ctx_t,
    xs0, xr0, xs1, xr1, us, ur, zs, zr, cz, fs, fin,
    row_of, col_of, ctx_of, live_of, user_in, item_in, ctx_in, insem,
    xsem, rsend, rrecv, qsend, qrecv, zsend, zrecv, psend, precv,
):
    blk = lax.axis_index("blk")
    r = lax.axis_index("rows")
    z, q = blk // NQ, lax.rem(blk, NQ)
    me = q * nr + r
    slots = xb.shape[0]
    members = NQ * nr
    groups = {
        "r": ring(nr, r, lambda i: (blk, i), False),
        "q": ring(NQ, q, lambda i: (z * NQ + i, r), False),
        "z": ring(nz, z, lambda i: (i * NQ + q, r), True),
        "p": plane(nr, q, r, lambda i: (z * NQ + i // nr, lax.rem(i, nr))),
    }
    semaphores = {
        "r": (rsend, rrecv), "q": (qsend, qrecv), "z": (zsend, zrecv), "p": (psend, precv),
    }

    pending = []
    used = {"r": 0, "q": 0, "z": 0, "p": 0}

    def exchange(kind, src, land, whole):
        send, recv = semaphores[kind]
        at = used[kind]
        used[kind] += 1
        e = Exchange(groups[kind], src, land, whole, send.at[at], recv.at[at])
        e.start()
        pending.append(e)
        return e

    barrier = pltpu.get_barrier_semaphore()
    for kind in ("z", "p"):
        steps, _, peer, dev = groups[kind]

        for i in range(steps):
            pl.semaphore_signal(
                barrier, inc=1, device_id=dev(peer(i)), device_id_type=MESH
            )

    inputs = [
        pltpu.make_async_copy(src, dst, insem.at[i])
        for i, (src, dst) in enumerate(
            (
                (item_hbm, item_in),
                (live_hbm, live_of),
                (col_hbm, col_of),
                (user_hbm, user_in),
                (row_hbm, row_of),
                (ctx_hbm, ctx_of),
                (factor_hbm, ctx_in),
            )
        )
    ]
    for c in inputs:
        c.start()
    load = pltpu.make_async_copy(blocks.at[0, 0], xb, xsem)
    load.start()
    for c in inputs:
        c.wait()
    live = live_of[0, 0]
    rows = [row_of[0, 0, s] for s in range(slots)]
    ctxs = [ctx_of[0, 0, s] for s in range(slots)]
    alive = [(s < live).astype(jnp.int32) for s in range(slots)]

    item_tiles = to_tiles(item_in[...])
    halves = [item_tiles, jnp.concatenate([item_tiles[:, 4:], item_tiles[:, :4]], axis=1)]
    ist[...] = jnp.stack(halves, axis=1).reshape(members, 8, 128)
    iq[q] = ist[me]
    sub = lax.broadcasted_iota(jnp.int32, (8, 128), 0)
    start = jnp.full((8, 128), -1000, jnp.int32)
    for s in range(slots):
        at = (col_of[0, 0, s] * 4) * alive[s] - 1000 * (1 - alive[s])
        start = jnp.where(sub == s, at, start)
    idx[me] = start
    user_own = user_in[...]
    gu[0, r] = user_own.astype(BF16)

    pl.semaphore_wait(barrier, nz - 1 + members - 1)

    item_first = exchange("q", lambda i: ist.at[i * nr + r], lambda i: iq.at[i], iq)
    index_gather = exchange("p", lambda i: idx.at[me], lambda i: idx.at[i], idx)
    item_first.wait()
    item_own = jnp.concatenate([iq[i][:4] for i in range(NQ)], axis=0)
    item_delta = jnp.zeros((16, 128), F32)
    zg[0, z] = item_own.astype(BF16)

    for k in range(ITERS):
        last = k == ITERS - 1
        z_gather = exchange("z", lambda i, k=k: zg.at[k, z], lambda i, k=k: zg.at[k, i], zg.at[k])
        if k == 0:
            user_gather = exchange("r", lambda i: gu.at[0, r], lambda i: gu.at[0, i], gu.at[0])
            for s in range(slots):
                w = ctx_in[...].astype(BF16).astype(F32)
                second = ctxs[s].astype(F32)
                wf[s] = w[:64] * (1.0 - second) + w[64:] * second
            index_gather.wait()
            sub3 = lax.broadcasted_iota(jnp.int32, (members, 8, 128), 1)
            row = [
                jnp.broadcast_to(idx[:, pl.ds(s, 1), :], (members, 8, 128)) for s in range(slots)
            ]
            first = jnp.where(sub3 < 4, row[0], row[1]) + lax.rem(sub3, 4)
            second = jnp.where(sub3 < 4, row[2], -1000) + lax.rem(sub3, 4)
            count = members * 16
            wanted = jnp.concatenate([first, second], axis=1).reshape(count, 128)
            total_rows = nz * 16
            lane = lax.broadcasted_iota(jnp.int32, (count, 128), 1)
            for c in range(total_rows // 128):
                hit = jnp.where(lane + 128 * c == wanted, 1.0, 0.0)
                bmat[:, 128 * c : 128 * (c + 1)] = hit.astype(BF16)
            at_row = lax.broadcasted_iota(jnp.int32, (total_rows, 128), 0)
            i0 = lax.broadcasted_iota(jnp.int32, (128, 128), 0)
            i1 = lax.broadcasted_iota(jnp.int32, (128, 128), 1)
            for c in range(count // 128):
                part = jnp.where(i0 == i1, wanted[128 * c : 128 * (c + 1)], 0)
                along = jnp.sum(part, axis=0, keepdims=True)
                hit = jnp.where(at_row == along, 1.0, 0.0)
                amat[:, 128 * c : 128 * (c + 1)] = hit.astype(BF16)
        z_gather.wait()
        shares = zg[k].reshape(nz * 16, 128)
        picked = jnp.dot(bmat[...], shares, preferred_element_type=F32)
        ys[k] = picked.astype(BF16).reshape(members, 16, 128)
        rg[k, me] = ys[k, me]
        answer = exchange("p", lambda i, k=k: ys.at[k, i], lambda i, k=k: rg.at[k, i], rg.at[k])
        user_gather.wait()
        for s in range(slots):
            total = jnp.zeros((64, 256), F32)
            for p in range(nr):
                total += gu[k, p].astype(F32) * (rows[s] == p).astype(jnp.int32).astype(F32)
            ub[s] = total.astype(BF16)
        user_t[...] = jnp.zeros_like(user_t)
        if last:
            ctx_t[...] = jnp.zeros_like(ctx_t)
        else:
            load.wait()
        answer.wait()
        got = rg[k].astype(F32)
        for s in range(slots):
            vf[s] = join_shares(got[:, 4 * s : 4 * s + 4, :])

        @pl.loop(0, 1)
        def _(c):
            for s in range(slots):
                u, w = ub[s], wf[s]
                v = vf[s, pl.ds(pl.multiple_of(c * 64, 64), 64), :]
                pair = (v.astype(BF16)[:, None, :] * w.astype(BF16)[None, :, :]).reshape(4096, 256)
                model = lax.dot_general(
                    u, pair, (((1,), (1,)), ((), ())), preferred_element_type=F32
                )
                x = xb[s, :, pl.ds(pl.multiple_of(c * 4096, 4096), 4096)]
                resid = (model - x.astype(F32)).astype(BF16)
                user_t[s] += jnp.dot(resid, pair, preferred_element_type=F32)
                g = lax.dot_general(
                    resid, u, (((0,), (0,)), ((), ())), preferred_element_type=F32
                ).reshape(64, 64, 256)
                item_t[s, pl.ds(pl.multiple_of(c * 64, 64), 64), :] = jnp.sum(g * w[None], axis=1)
                if last:
                    ctx_t[s] += jnp.sum(g * v[:, None, :], axis=0)

        xs, xr = (xs1, xr1) if last else (xs0, xr0)
        tiles = [to_tiles(item_t[s]) for s in range(slots)]
        fill = jnp.zeros((16, 4, 128), F32)
        for half in range(2):
            cut = [t[:, 4 * half : 4 * half + 4] for t in tiles]
            part = jnp.concatenate(cut + [fill], axis=1).astype(BF16)
            for v in range(16):
                xs[2 * v + half, pl.ds(0, 16), :] = part[v]
        if last:
            for c in range(2):
                total = jnp.zeros((64, 256), F32)
                for s in range(slots):
                    mine = alive[s] * (ctxs[s] == c).astype(jnp.int32)
                    total += ctx_t[s] * mine.astype(F32)
                part = to_tiles(total)
                part = jnp.concatenate([part, jnp.zeros_like(part)], axis=1).astype(BF16)
                xs[pl.ds(16 * c, 16), pl.ds(16, 16), :] = part
        xr[me] = xs[me]
        item_parts = exchange("p", lambda i, xs=xs: xs.at[i], lambda i, xr=xr: xr.at[i], xr)
        for p in range(nr):
            total = jnp.zeros((64, 256), F32)
            for s in range(slots):
                mine = alive[s] * (rows[s] == p).astype(jnp.int32)
                total += user_t[s] * mine.astype(F32)
            us[k, p] = total.astype(BF16)
        ur[k, r] = us[k, r]
        user_parts = exchange("r", lambda i, k=k: us.at[k, i], lambda i, k=k: ur.at[k, i], ur.at[k])

        item_parts.wait()
        parts = xr[:, :16, :].reshape(members * 16, 128)
        summed = jnp.dot(amat[...], parts, preferred_element_type=F32)
        zs[k] = summed.astype(BF16).reshape(nz, 16, 128)
        zr[k, z] = zs[k, z]
        z_parts = exchange("z", lambda i, k=k: zs.at[k, i], lambda i, k=k: zr.at[k, i], zr.at[k])
        if last:
            cz[z] = jnp.sum(xr[:, 16:, :].astype(F32), axis=0)[:8]
            ctx_z = exchange("z", lambda i: cz.at[z], lambda i: cz.at[i], cz)
        user_parts.wait()
        user_own = user_own - user_step * jnp.sum(ur[k].astype(F32), axis=0)
        if last:
            new_users[...] = user_own
        else:
            gu[k + 1, r] = user_own.astype(BF16)
            user_gather = exchange(
                "r", lambda i, k=k: gu.at[k + 1, r], lambda i, k=k: gu.at[k + 1, i], gu.at[k + 1])
        z_parts.wait()
        item_delta = item_delta + item_step * jnp.sum(zr[k].astype(F32), axis=0)
        if not last:
            zg[k + 1, z] = (item_own - item_delta).astype(BF16)

    ctx_z.wait()
    ctx_share = jnp.sum(cz[...], axis=0) * grad_scale
    for i in range(NQ):
        part = item_delta[4 * i : 4 * i + 4]
        rest = part - part.astype(BF16).astype(F32)
        fs[i] = jnp.concatenate([part, rest, ctx_share], axis=0).astype(BF16)
    fin[me] = fs[q]
    final = exchange("p", lambda i: fs.at[i // nr], lambda i: fin.at[i], fin)
    final.wait()
    got = fin[...].astype(F32)
    new_items[...] = item_in[...] - join_shares(got[:, :4] + got[:, 4:8])
    for c in range(2):
        ctx_out[pl.ds(64 * c, 64), :] = from_tiles(got[16 * c : 16 * c + 16, 8:])
    for e in pending:
        e.finish()


def local(
    blocks, block_row, block_col, block_ctx, live_blocks, user_factor, item_factor, context_factor
):
    nr = lax.axis_size("rows")
    nz = lax.axis_size("blk") // NQ
    slots = blocks.shape[2]
    nb = nz * NQ
    edge = blocks.shape[3]
    vm = pltpu.VMEM
    dma = pltpu.SemaphoreType.DMA
    members = NQ * nr
    scratch = [
        vm((slots, 64, 4096), BF16),
        vm((ITERS, nr, 64, 256), BF16),
        vm((members, 8, 128), jnp.int32),
        vm((members * 16, nz * 16), BF16),
        vm((nz * 16, members * 16), BF16),
        vm((NQ, 8, 128), F32),
        vm((members, 8, 128), F32),
        vm((ITERS, nz, 16, 128), BF16),
        vm((ITERS, members, 16, 128), BF16),
        vm((ITERS, members, 16, 128), BF16),
        vm((slots, 64, 256), F32),
        vm((slots, 64, 256), F32),
        vm((slots, 64, 256), BF16),
        vm((slots, 64, 256), F32),
        vm((slots, 64, 256), F32),
        vm((slots, 64, 256), F32),
        vm((members, 16, 128), BF16),
        vm((members, 16, 128), BF16),
        vm((members, 32, 128), BF16),
        vm((members, 32, 128), BF16),
        vm((ITERS, nr, 64, 256), BF16),
        vm((ITERS, nr, 64, 256), BF16),
        vm((ITERS, nz, 16, 128), BF16),
        vm((ITERS, nz, 16, 128), BF16),
        vm((nz, 8, 128), F32),
        vm((NQ, 16, 128), BF16),
        vm((members, 16, 128), BF16),
        pltpu.SMEM((1, 1, slots), jnp.int32),
        pltpu.SMEM((1, 1, slots), jnp.int32),
        pltpu.SMEM((1, 1, slots), jnp.int32),
        pltpu.SMEM((1, 1), jnp.int32),
        vm((64, 256), F32),
        vm((64, 256), F32),
        vm((128, 256), F32),
        dma((7,)),
        dma,
        dma((4,)),
        dma((4,)),
        dma((1,)),
        dma((1,)),
        dma((5,)),
        dma((5,)),
        dma((6,)),
        dma((6,)),
    ]
    body = functools.partial(
        kernel,
        nz,
        nr,
        6.4 / (edge * edge),
        16.0 / (edge * edge * nr),
        8.0 / (edge * math.sqrt(nb * nr)),
    )
    in_vmem = pl.BlockSpec(memory_space=pltpu.VMEM)
    return pl.pallas_call(
        body,
        out_shape=(
            jax.ShapeDtypeStruct(user_factor.shape, F32),
            jax.ShapeDtypeStruct(item_factor.shape, F32),
            jax.ShapeDtypeStruct(context_factor.shape, F32),
        ),
        in_specs=[pl.BlockSpec(memory_space=pltpu.HBM)] * 8,
        out_specs=(in_vmem,) * 3,
        scratch_shapes=scratch,
        compiler_params=pltpu.CompilerParams(
            collective_id=0, has_side_effects=True, vmem_limit_bytes=56 * 1024 * 1024
        ),
    )(
        blocks, block_row, block_col, block_ctx, live_blocks,
        user_factor, item_factor, context_factor,
    )


def solution(mesh):
    return jax.shard_map(
        local,
        mesh=mesh,
        in_specs=(
            P("blk", "rows", None, None, None),
            P("blk", "rows", None),
            P("blk", "rows", None),
            P("blk", "rows", None),
            P("blk", "rows"),
            P(("blk", "rows"), None),
            P("blk", None),
            P(),
        ),
        out_specs=(P(("blk", "rows"), None), P("blk", None), P()),
        check_vma=False,
    )
```

```python
import functools
import math

import jax
import jax.numpy as jnp
from jax import lax
from jax.experimental import pallas as pl
from jax.experimental.pallas import tpu as pltpu
from jax.sharding import PartitionSpec as P

ITERS = 2
NQ = 4
MESH = pl.DeviceIdType.MESH
F32 = jnp.float32
BF16 = jnp.bfloat16


class Exchange:
    def __init__(self, group, src, land, whole, send, recv):
        self.steps, self.me, self.peer, self.dev = group
        self.src, self.land, self.whole, self.send, self.recv = src, land, whole, send, recv

    def start(self):
        for i in range(self.steps):
            to = self.peer(i)
            pltpu.make_async_remote_copy(
                src_ref=self.src(to),
                dst_ref=self.land(self.me),
                send_sem=self.send,
                recv_sem=self.recv,
                device_id=self.dev(to),
                device_id_type=MESH,
            ).start()

    def _all(self):
        part = self.whole.at[pl.ds(0, self.steps)]
        return pltpu.make_async_remote_copy(
            src_ref=part,
            dst_ref=part,
            send_sem=self.send,
            recv_sem=self.recv,
            device_id=self.dev(self.peer(0)),
            device_id_type=MESH,
        )

    def wait(self):
        self._all().wait_recv()

    def finish(self):
        self._all().wait_send()


def ring(n, me, dev, far_first):
    def offset(i):
        if not far_first:
            return i + 1
        return n // 2 + (1 - 2 * (i % 2)) * ((i + 1) // 2)

    return (
        n - 1,
        me,
        lambda i: lax.rem(me + offset(i), n),
        dev,
    )


def plane(nr, q, r, dev):
    y_lo, core, y_hi, x = q // 2, lax.rem(q, 2), r // 4, lax.rem(r, 4)
    n = NQ * nr

    xs = [lax.rem(x + d, 4) for d in range(4)]
    his = [y_hi * 4, (1 - y_hi) * 4]
    qs = [
        (lo * 2 + c) * nr for lo in (y_lo, 1 - y_lo) for c in (core, 1 - core)
    ]
    rows = [hi + xx for hi in his for xx in xs]
    hops = [(dhi * 2 if not dlo else 1) + min(d, 4 - d) + dlo * (1 - dhi)
            for dlo in range(2) for dhi in range(2) for d in range(4)]
    order = sorted(
        (-hops[(dlo * 2 + dhi) * 4 + d], dlo * 2 + c, dhi * 4 + d)
        for dlo in range(2) for c in range(2) for dhi in range(2) for d in range(4)
    )
    steps = [(a, b) for _, a, b in order if (a, b) != (0, 0)]

    def member(i):
        a, b = steps[i]
        return qs[a] + rows[b]

    return (n - 1, q * nr + r, member, dev)


def to_tiles(x):
    y = x.reshape(8, 8, 256)
    return jnp.stack([y[..., :128], y[..., 128:]], axis=1).reshape(16, 8, 128)


def from_tiles(x):
    y = x.reshape(8, 2, 8, 128)
    return jnp.concatenate([y[:, 0], y[:, 1]], axis=-1).reshape(64, 256)


def join_shares(x):
    y = x.reshape(16, 2, 4, 128)
    return from_tiles(jnp.concatenate([y[:, 0], y[:, 1]], axis=1))


def kernel(
    nz, nr, user_step, item_step, grad_scale,
    blocks, row_hbm, col_hbm, ctx_hbm, live_hbm, user_hbm, item_hbm, factor_hbm,
    new_users, new_items, ctx_out,
    xb, gu, idx, bmat, amat, iq, ist, zg, ys, rg, vf, wf, ub, user_t, item_t, ctx_t,
    xs0, xr0, xs1, xr1, us, ur, zs, zr, cz, fs, fin,
    row_of, col_of, ctx_of, live_of, user_in, item_in, ctx_in, insem,
    xsem, rsend, rrecv, qsend, qrecv, zsend, zrecv, psend, precv,
):
    blk = lax.axis_index("blk")
    r = lax.axis_index("rows")
    z, q = blk // NQ, lax.rem(blk, NQ)
    me = q * nr + r
    slots = xb.shape[0]
    members = NQ * nr
    groups = {
        "r": ring(nr, r, lambda i: (blk, i), False),
        "q": ring(NQ, q, lambda i: (z * NQ + i, r), False),
        "z": ring(nz, z, lambda i: (i * NQ + q, r), True),
        "p": plane(nr, q, r, lambda i: (z * NQ + i // nr, lax.rem(i, nr))),
    }
    semaphores = {
        "r": (rsend, rrecv), "q": (qsend, qrecv), "z": (zsend, zrecv), "p": (psend, precv),
    }

    pending = []
    used = {"r": 0, "q": 0, "z": 0, "p": 0}

    def exchange(kind, src, land, whole):
        send, recv = semaphores[kind]
        at = used[kind]
        used[kind] += 1
        e = Exchange(groups[kind], src, land, whole, send.at[at], recv.at[at])
        e.start()
        pending.append(e)
        return e

    barrier = pltpu.get_barrier_semaphore()
    for kind in ("z", "p"):
        steps, _, peer, dev = groups[kind]

        for i in range(steps):
            pl.semaphore_signal(
                barrier, inc=1, device_id=dev(peer(i)), device_id_type=MESH
            )

    inputs = [
        pltpu.make_async_copy(src, dst, insem.at[i])
        for i, (src, dst) in enumerate(
            (
                (item_hbm, item_in),
                (live_hbm, live_of),
                (col_hbm, col_of),
                (user_hbm, user_in),
                (row_hbm, row_of),
                (ctx_hbm, ctx_of),
                (factor_hbm, ctx_in),
            )
        )
    ]
    for c in inputs:
        c.start()
    load = pltpu.make_async_copy(blocks.at[0, 0], xb, xsem)
    load.start()
    for c in inputs:
        c.wait()
    live = live_of[0, 0]
    rows = [row_of[0, 0, s] for s in range(slots)]
    ctxs = [ctx_of[0, 0, s] for s in range(slots)]
    alive = [(s < live).astype(jnp.int32) for s in range(slots)]

    item_tiles = to_tiles(item_in[...])
    halves = [item_tiles, jnp.concatenate([item_tiles[:, 4:], item_tiles[:, :4]], axis=1)]
    ist[...] = jnp.stack(halves, axis=1).reshape(members, 8, 128)
    iq[q] = ist[me]
    sub = lax.broadcasted_iota(jnp.int32, (8, 128), 0)
    start = jnp.full((8, 128), -1000, jnp.int32)
    for s in range(slots):
        at = (col_of[0, 0, s] * 4) * alive[s] - 1000 * (1 - alive[s])
        start = jnp.where(sub == s, at, start)
    idx[me] = start
    user_own = user_in[...]
    gu[0, r] = user_own.astype(BF16)

    pl.semaphore_wait(barrier, nz - 1 + members - 1)

    item_first = exchange("q", lambda i: ist.at[i * nr + r], lambda i: iq.at[i], iq)
    index_gather = exchange("p", lambda i: idx.at[me], lambda i: idx.at[i], idx)
    item_first.wait()
    item_own = jnp.concatenate([iq[i][:4] for i in range(NQ)], axis=0)
    item_delta = jnp.zeros((16, 128), F32)
    zg[0, z] = item_own.astype(BF16)

    for k in range(ITERS):
        last = k == ITERS - 1
        z_gather = exchange("z", lambda i, k=k: zg.at[k, z], lambda i, k=k: zg.at[k, i], zg.at[k])
        if k == 0:
            user_gather = exchange("r", lambda i: gu.at[0, r], lambda i: gu.at[0, i], gu.at[0])
            for s in range(slots):
                w = ctx_in[...].astype(BF16).astype(F32)
                second = ctxs[s].astype(F32)
                wf[s] = w[:64] * (1.0 - second) + w[64:] * second
            index_gather.wait()
            sub3 = lax.broadcasted_iota(jnp.int32, (members, 8, 128), 1)
            row = [
                jnp.broadcast_to(idx[:, pl.ds(s, 1), :], (members, 8, 128)) for s in range(slots)
            ]
            first = jnp.where(sub3 < 4, row[0], row[1]) + lax.rem(sub3, 4)
            second = jnp.where(sub3 < 4, row[2], -1000) + lax.rem(sub3, 4)
            count = members * 16
            wanted = jnp.concatenate([first, second], axis=1).reshape(count, 128)
            total_rows = nz * 16
            lane = lax.broadcasted_iota(jnp.int32, (count, 128), 1)
            for c in range(total_rows // 128):
                hit = jnp.where(lane + 128 * c == wanted, 1.0, 0.0)
                bmat[:, 128 * c : 128 * (c + 1)] = hit.astype(BF16)
            at_row = lax.broadcasted_iota(jnp.int32, (total_rows, 128), 0)
            i0 = lax.broadcasted_iota(jnp.int32, (128, 128), 0)
            i1 = lax.broadcasted_iota(jnp.int32, (128, 128), 1)
            for c in range(count // 128):
                part = jnp.where(i0 == i1, wanted[128 * c : 128 * (c + 1)], 0)
                along = jnp.sum(part, axis=0, keepdims=True)
                hit = jnp.where(at_row == along, 1.0, 0.0)
                amat[:, 128 * c : 128 * (c + 1)] = hit.astype(BF16)
        z_gather.wait()
        shares = zg[k].reshape(nz * 16, 128)
        picked = jnp.dot(bmat[...], shares, preferred_element_type=F32)
        ys[k] = picked.astype(BF16).reshape(members, 16, 128)
        rg[k, me] = ys[k, me]
        answer = exchange("p", lambda i, k=k: ys.at[k, i], lambda i, k=k: rg.at[k, i], rg.at[k])
        user_gather.wait()
        for s in range(slots):
            total = jnp.zeros((64, 256), F32)
            for p in range(nr):
                total += gu[k, p].astype(F32) * (rows[s] == p).astype(jnp.int32).astype(F32)
            ub[s] = total.astype(BF16)
        user_t[...] = jnp.zeros_like(user_t)
        if last:
            ctx_t[...] = jnp.zeros_like(ctx_t)
        else:
            load.wait()
        answer.wait()
        got = rg[k].astype(F32)
        for s in range(slots):
            vf[s] = join_shares(got[:, 4 * s : 4 * s + 4, :])

        @pl.loop(0, 1)
        def _(c):
            for s in range(slots):
                u, w = ub[s], wf[s]
                v = vf[s, pl.ds(pl.multiple_of(c * 64, 64), 64), :]
                pair = (v.astype(BF16)[:, None, :] * w.astype(BF16)[None, :, :]).reshape(4096, 256)
                model = lax.dot_general(
                    u, pair, (((1,), (1,)), ((), ())), preferred_element_type=F32
                )
                x = xb[s, :, pl.ds(pl.multiple_of(c * 4096, 4096), 4096)]
                resid = (model - x.astype(F32)).astype(BF16)
                user_t[s] += jnp.dot(resid, pair, preferred_element_type=F32)
                g = lax.dot_general(
                    resid, u, (((0,), (0,)), ((), ())), preferred_element_type=F32
                ).reshape(64, 64, 256)
                item_t[s, pl.ds(pl.multiple_of(c * 64, 64), 64), :] = jnp.sum(g * w[None], axis=1)
                if last:
                    ctx_t[s] += jnp.sum(g * v[:, None, :], axis=0)

        xs, xr = (xs1, xr1) if last else (xs0, xr0)
        tiles = [to_tiles(item_t[s]) for s in range(slots)]
        fill = jnp.zeros((16, 4, 128), F32)
        for half in range(2):
            cut = [t[:, 4 * half : 4 * half + 4] for t in tiles]
            part = jnp.concatenate(cut + [fill], axis=1).astype(BF16)
            for v in range(16):
                xs[2 * v + half, pl.ds(0, 16), :] = part[v]
        if last:
            for c in range(2):
                total = jnp.zeros((64, 256), F32)
                for s in range(slots):
                    mine = alive[s] * (ctxs[s] == c).astype(jnp.int32)
                    total += ctx_t[s] * mine.astype(F32)
                part = to_tiles(total)
                part = jnp.concatenate([part, jnp.zeros_like(part)], axis=1).astype(BF16)
                xs[pl.ds(16 * c, 16), pl.ds(16, 16), :] = part
        xr[me] = xs[me]
        item_parts = exchange("p", lambda i, xs=xs: xs.at[i], lambda i, xr=xr: xr.at[i], xr)
        item_parts.wait()
        parts = xr[:, :16, :].reshape(members * 16, 128)
        summed = jnp.dot(amat[...], parts, preferred_element_type=F32)
        zs[k] = summed.astype(BF16).reshape(nz, 16, 128)
        zr[k, z] = zs[k, z]
        z_parts = exchange("z", lambda i, k=k: zs.at[k, i], lambda i, k=k: zr.at[k, i], zr.at[k])
        if last:
            cz[z] = jnp.sum(xr[:, 16:, :].astype(F32), axis=0)[:8]
            ctx_z = exchange("z", lambda i: cz.at[z], lambda i: cz.at[i], cz)
        for p in range(nr):
            total = jnp.zeros((64, 256), F32)
            for s in range(slots):
                mine = alive[s] * (rows[s] == p).astype(jnp.int32)
                total += user_t[s] * mine.astype(F32)
            us[k, p] = total.astype(BF16)
        ur[k, r] = us[k, r]
        user_parts = exchange("r", lambda i, k=k: us.at[k, i], lambda i, k=k: ur.at[k, i], ur.at[k])
        user_parts.wait()
        user_own = user_own - user_step * jnp.sum(ur[k].astype(F32), axis=0)
        if last:
            new_users[...] = user_own
        else:
            gu[k + 1, r] = user_own.astype(BF16)
            user_gather = exchange(
                "r", lambda i, k=k: gu.at[k + 1, r], lambda i, k=k: gu.at[k + 1, i], gu.at[k + 1])
        z_parts.wait()
        item_delta = item_delta + item_step * jnp.sum(zr[k].astype(F32), axis=0)
        if not last:
            zg[k + 1, z] = (item_own - item_delta).astype(BF16)

    ctx_z.wait()
    ctx_share = jnp.sum(cz[...], axis=0) * grad_scale
    for i in range(NQ):
        part = item_delta[4 * i : 4 * i + 4]
        rest = part - part.astype(BF16).astype(F32)
        fs[i] = jnp.concatenate([part, rest, ctx_share], axis=0).astype(BF16)
    fin[me] = fs[q]
    final = exchange("p", lambda i: fs.at[i // nr], lambda i: fin.at[i], fin)
    final.wait()
    got = fin[...].astype(F32)
    new_items[...] = item_in[...] - join_shares(got[:, :4] + got[:, 4:8])
    for c in range(2):
        ctx_out[pl.ds(64 * c, 64), :] = from_tiles(got[16 * c : 16 * c + 16, 8:])
    for e in pending:
        e.finish()


def local(
    blocks, block_row, block_col, block_ctx, live_blocks, user_factor, item_factor, context_factor
):
    nr = lax.axis_size("rows")
    nz = lax.axis_size("blk") // NQ
    slots = blocks.shape[2]
    nb = nz * NQ
    edge = blocks.shape[3]
    vm = pltpu.VMEM
    dma = pltpu.SemaphoreType.DMA
    members = NQ * nr
    scratch = [
        vm((slots, 64, 4096), BF16),
        vm((ITERS, nr, 64, 256), BF16),
        vm((members, 8, 128), jnp.int32),
        vm((members * 16, nz * 16), BF16),
        vm((nz * 16, members * 16), BF16),
        vm((NQ, 8, 128), F32),
        vm((members, 8, 128), F32),
        vm((ITERS, nz, 16, 128), BF16),
        vm((ITERS, members, 16, 128), BF16),
        vm((ITERS, members, 16, 128), BF16),
        vm((slots, 64, 256), F32),
        vm((slots, 64, 256), F32),
        vm((slots, 64, 256), BF16),
        vm((slots, 64, 256), F32),
        vm((slots, 64, 256), F32),
        vm((slots, 64, 256), F32),
        vm((members, 16, 128), BF16),
        vm((members, 16, 128), BF16),
        vm((members, 32, 128), BF16),
        vm((members, 32, 128), BF16),
        vm((ITERS, nr, 64, 256), BF16),
        vm((ITERS, nr, 64, 256), BF16),
        vm((ITERS, nz, 16, 128), BF16),
        vm((ITERS, nz, 16, 128), BF16),
        vm((nz, 8, 128), F32),
        vm((NQ, 16, 128), BF16),
        vm((members, 16, 128), BF16),
        pltpu.SMEM((1, 1, slots), jnp.int32),
        pltpu.SMEM((1, 1, slots), jnp.int32),
        pltpu.SMEM((1, 1, slots), jnp.int32),
        pltpu.SMEM((1, 1), jnp.int32),
        vm((64, 256), F32),
        vm((64, 256), F32),
        vm((128, 256), F32),
        dma((7,)),
        dma,
        dma((4,)),
        dma((4,)),
        dma((1,)),
        dma((1,)),
        dma((5,)),
        dma((5,)),
        dma((6,)),
        dma((6,)),
    ]
    body = functools.partial(
        kernel,
        nz,
        nr,
        6.4 / (edge * edge),
        16.0 / (edge * edge * nr),
        8.0 / (edge * math.sqrt(nb * nr)),
    )
    in_vmem = pl.BlockSpec(memory_space=pltpu.VMEM)
    return pl.pallas_call(
        body,
        out_shape=(
            jax.ShapeDtypeStruct(user_factor.shape, F32),
            jax.ShapeDtypeStruct(item_factor.shape, F32),
            jax.ShapeDtypeStruct(context_factor.shape, F32),
        ),
        in_specs=[pl.BlockSpec(memory_space=pltpu.HBM)] * 8,
        out_specs=(in_vmem,) * 3,
        scratch_shapes=scratch,
        compiler_params=pltpu.CompilerParams(
            collective_id=0, has_side_effects=True, vmem_limit_bytes=56 * 1024 * 1024
        ),
    )(
        blocks, block_row, block_col, block_ctx, live_blocks,
        user_factor, item_factor, context_factor,
    )


def solution(mesh):
    return jax.shard_map(
        local,
        mesh=mesh,
        in_specs=(
            P("blk", "rows", None, None, None),
            P("blk", "rows", None),
            P("blk", "rows", None),
            P("blk", "rows", None),
            P("blk", "rows"),
            P(("blk", "rows"), None),
            P("blk", None),
            P(),
        ),
        out_specs=(P(("blk", "rows"), None), P("blk", None), P()),
        check_vma=False,
    )
```
